256 devices in a mesh: dp: 8 (over y, x_hi), seq: 32 (over x_lo, z, core).
Axes of the slice: x: 4 (x_hi: 2, x_lo: 2; x = x_hi * 2 + x_lo), y: 4, z: 8, core: 2. Of those that a mesh axis runs over, the one named last changes fastest.
Arguments:
- frames_in: bfloat16 [65536, 1536], P(('dp', 'seq')), parts along dimension 0, may hold values from -3 to 3
- queries: bfloat16 [65536, 768], P(('dp', 'seq')), parts along dimension 0, may hold values from -24 to 24
- keys: bfloat16 [65536, 768], P(('dp', 'seq')), parts along dimension 0, may hold values from -6 to 6
- values: bfloat16 [65536, 768], P(('dp', 'seq')), parts along dimension 0, may hold values from -6 to 6
- w_out: bfloat16 [768, 1536], replicated, may hold values from -0.21875 to 0.21875
- ln_gain: float32 [1536], replicated, may hold values from 0.5 to 1.5
- w_glu: bfloat16 [1536, 1536], replicated, may hold values from -0.15625 to 0.15625
- dw_weight: float32 [31, 768], replicated, may hold values from -1 to 1
- bn_scale: float32 [768], replicated, may hold values from 0.5 to 2
- bn_shift: float32 [768], replicated, may hold values from -2 to 2
Outputs:
- attended: bfloat16 [65536, 1536], P(('dp', 'seq')), parts along dimension 0
- conv_out: bfloat16 [65536, 768], P(('dp', 'seq')), parts along dimension 0
The draws below stay inside these ranges and needn't reach their ends.
There are 8 independent parts, one for each index of `dp`. The reference program is written for one: setup_inputs(seed, part) draws one part's arguments, and reference() takes and returns one part's arrays. A program takes and returns all parts, laid end to end along the dimension named above; an argument that names none is the same for every part. Nothing has to cross between parts.
All inputs are finite; a program needn't handle non-finite values.
Results may differ from the reference program's by a relative error of at most 0.013.
Values may be sent and summed in bfloat16 or wider, within the bound.
A program may use at most 128 MiB of HBM per device.

```python
import math
import jax
import jax.numpy as jnp
from jax import lax

D = 1536
HEADS = 12
HD = 64
CH = 768
TAPS = 31
HW = 768
FRAMES = 8192


def draw_queries(key, part):
    key = jax.random.fold_in(key, 11)
    result = jnp.clip(1.5 * jax.random.normal(key, (FRAMES, HW), jnp.float32), -6.0, 6.0)
    return result.astype(jnp.bfloat16)


def draw_keys(key, part):
    key = jax.random.fold_in(key, 23)
    result = jnp.clip(1.5 * jax.random.normal(key, (FRAMES, HW), jnp.float32), -6.0, 6.0)
    return result.astype(jnp.bfloat16)


def levels(stream_key, shape, pieces, smallest, high):
    def one(position, blocks):
        steps = jax.random.uniform(jax.random.fold_in(jax.random.fold_in(stream_key, 6), position), (blocks,), jnp.float32, smallest / len(pieces), high / len(pieces))
        return jnp.repeat(jnp.exp(steps), shape[position] // blocks).reshape((-1,) + (1,) * (len(shape) - position - 1))

    gain = one(*pieces[0])
    for cut in pieces[1:]:
        gain = gain * one(*cut)
    return gain


def gaussian(key, shape, deviation, bound, split=(), kind=jnp.bfloat16):
    values = deviation * jax.random.normal(key, shape, jnp.float32)
    if split:
        values = values * levels(key, shape, split, -0.22, 0.18)
    return jnp.clip(values, -bound, bound).astype(kind)


def setup_inputs(seed: int = 0, part: int = 0) -> dict:
    key_list = jax.random.split(jax.random.key(seed), 11)
    part_splits = jax.random.split(jax.random.fold_in(key_list[10], part), 11)
    frames_in = gaussian(part_splits[0], (FRAMES, D), 0.5, 3.0, ((0, 32),))
    queries = draw_queries(jax.random.fold_in(jax.random.fold_in(key_list[10], part), 71), part)
    keys = draw_keys(jax.random.fold_in(jax.random.fold_in(key_list[10], part), 71), part)
    values = gaussian(part_splits[3], (FRAMES, HW), 1.0, 6.0, ((0, 32),))
    w_out = gaussian(key_list[4], (HW, D), HW ** -0.5, 0.21875)
    ln_gain = jnp.clip(jax.random.uniform(key_list[5], (D,), jnp.float32, 0.5, 1.5), 0.5, 1.5)
    w_glu = gaussian(key_list[6], (D, 2 * CH), D ** -0.5, 0.15625)
    dw_weight = gaussian(key_list[7], (TAPS, CH), TAPS ** -0.5, 1.0, (), jnp.float32)
    bn_scale = jnp.clip(jnp.exp(jax.random.uniform(key_list[8], (CH,), jnp.float32, math.log(0.5), math.log(2.0))), 0.5, 2.0)
    bn_shift = gaussian(key_list[9], (CH,), 0.5, 2.0, (), jnp.float32)
    return dict(frames_in=frames_in, queries=queries, keys=keys, values=values, w_out=w_out, ln_gain=ln_gain, w_glu=w_glu, dw_weight=dw_weight, bn_scale=bn_scale, bn_shift=bn_shift)


def head_attention(query_head, key_head, value_head):
    length = query_head.shape[0]
    block = math.gcd(length, 512)
    key_float = key_head.astype(jnp.float32)
    value_float = value_head.astype(jnp.float32)
    scale = 1.0 / math.sqrt(HD)
    blocks = query_head.astype(jnp.float32).reshape(length // block, block, HD)

    def one_block(query_block):
        scores = jnp.dot(query_block, key_float.T, precision=lax.Precision.HIGHEST) * scale
        row_max = lax.optimization_barrier(jnp.max(scores, axis=1, keepdims=True))
        weights = jnp.exp(scores - row_max)
        rounded = lax.optimization_barrier(weights.astype(jnp.bfloat16)).astype(jnp.float32)
        context = jnp.dot(rounded, value_float, precision=lax.Precision.HIGHEST)
        return context / lax.optimization_barrier(jnp.sum(weights, axis=1, keepdims=True))
    return lax.map(one_block, blocks).reshape(length, HD)

def reference(frames_in, queries, keys, values, w_out, ln_gain, w_glu, dw_weight, bn_scale, bn_shift):
    length = queries.shape[0]

    def split_heads(array):
        return array.reshape(length, HEADS, HD).transpose(1, 0, 2)
    per_head = lax.map(lambda triple: head_attention(triple[0], triple[1], triple[2]), (split_heads(queries), split_heads(keys), split_heads(values)))
    context = per_head.transpose(1, 0, 2).reshape(length, HEADS * HD).astype(jnp.bfloat16)
    residual_sum = frames_in.astype(jnp.float32) + jnp.dot(context, w_out, preferred_element_type=jnp.float32)
    attended = residual_sum.astype(jnp.bfloat16)
    mean_value = lax.optimization_barrier(jnp.mean(residual_sum, axis=1, keepdims=True))
    centered = residual_sum - mean_value
    variance = lax.optimization_barrier(jnp.mean(centered * centered, axis=1, keepdims=True))
    normed = (centered / jnp.sqrt(variance + 1e-05) * ln_gain).astype(jnp.bfloat16)
    projected = jnp.dot(normed, w_glu, preferred_element_type=jnp.float32)
    gated = (projected[:, :CH] * jax.nn.sigmoid(projected[:, CH:])).astype(jnp.bfloat16)
    half_width = TAPS // 2
    padded = jnp.pad(gated, ((half_width, half_width), (0, 0)))
    conv = jnp.zeros((length, CH), jnp.float32)
    for tap_index in range(TAPS):
        conv = conv + padded[tap_index:tap_index + length].astype(jnp.float32) * dw_weight[tap_index]
    shifted = bn_scale * conv + bn_shift
    conv_out = (shifted * jax.nn.sigmoid(shifted)).astype(jnp.bfloat16)
    return (attended, conv_out)
```

```python
import jax
import jax.numpy as jnp
from jax import lax
from jax.experimental import pallas as pl
from jax.experimental.pallas import tpu as pltpu
from jax.sharding import PartitionSpec as P

MESH = pl.DeviceIdType.MESH
BF16 = jnp.bfloat16
F32 = jnp.float32

HD = 64
TAPS = 31
ROWS = 256
Z = 8
BLOCKS = 12
CHUNK = 1024
EXP_SCALE = 0.125 * 1.4426950408889634

OWN_SLOT = (10, 7, 4, 1, 0, 2, 5, 8)
SHARED_SLOT = (11, 9, 6, 3)
UNROLL = 4


def kernel(
    frames_hbm, q_ref, k_ref, v_ref, wout_hbm, gain_ref, wglu_hbm, dw_ref, bns_ref, bnb_ref,
    att_ref, conv_ref,
    kv_send, q_send, kv, qb, ctx_send, ctx_t, s_scr, mx_scr, m_scr, acc_scr,
    frames, wout, wglu, gpad, taps_tmp, halo_send, halo_recv,
    local_sem, q_ssem, q_rsem, z_ssem, z_rsem, a_ssem, a_rsem, x_ssem, x_rsem, b_ssem, b_rsem,
    c_ssem, c_rsem, h_ssem, h_rsem,
):
    me = lax.axis_index("seq")
    x, z, c = me // 16, lax.rem(me // 2, Z), lax.rem(me, 2)
    odd = lax.rem(z, 2)
    slab = 2 * x + c

    def dev(x, z, c):
        return {"seq": (x * Z + z) * 2 + c}

    def along_z(step):
        return lax.rem(z + step + Z, Z)

    sibling = dev(x, z, 1 - c)
    across = dev(1 - x, z, c)
    left = {"seq": lax.rem(me + 31, 32)}
    right = {"seq": lax.rem(me + 1, 32)}
    other = {"seq": jnp.where(c == 1, lax.rem(me + 1, 32), lax.rem(me + 31, 32))}

    def remote(src, dst, ssem, rsem, to):
        return pltpu.make_async_remote_copy(
            src_ref=src, dst_ref=dst, send_sem=ssem, recv_sem=rsem, device_id=to, device_id_type=MESH
        )

    loads = [
        pltpu.make_async_copy(frames_hbm, frames, local_sem.at[0]),
        pltpu.make_async_copy(wout_hbm, wout, local_sem.at[1]),
        pltpu.make_async_copy(wglu_hbm, wglu, local_sem.at[2]),
    ]
    for load in loads:
        load.start()

    qb[...] = jnp.zeros_like(qb)
    barrier = pltpu.get_barrier_semaphore()
    peers = [dev(x, along_z(d), c) for d in range(1, Z)] + [sibling, across, other]
    for peer in peers:
        pl.semaphore_signal(barrier, inc=1, device_id=peer, device_id_type=MESH)

    q_send[...] = q_ref[...].T.reshape(q_send.shape)
    v_t = v_ref[...].T
    k_all = k_ref[...]
    for zz in range(Z):
        own, shared = 3 * (zz // 2) + 2 * (zz % 2), 3 * (zz // 2) + 1
        kv_send[zz, :ROWS, :] = jnp.concatenate(
            [k_all[:, h * HD : (h + 1) * HD] for h in (own, shared)], axis=1
        )
        v_pair = jnp.concatenate([v_t[h * HD : (h + 1) * HD] for h in (own, shared)], axis=0)
        kv_send[zz, ROWS : ROWS + 128, :] = v_pair[:, :128]
        kv_send[zz, ROWS + 128 :, :] = v_pair[:, 128:]

    def own_head(zz):
        return 3 * (zz // 2) + 2 * lax.rem(zz, 2)

    def shared_head(zz):
        return 3 * (zz // 2) + 1

    def shared_step(i):
        return jnp.where(lax.rem(z + i, 2) == 0, i, -i)

    def home_step(i):
        return jnp.where(odd == 1, i, -i)

    qb[OWN_SLOT[0], :HD, :] = q_send[own_head(z)]
    qb[SHARED_SLOT[0], HD:, :] = q_send[shared_head(z)]
    kv[0, slab] = kv_send[z]

    pl.semaphore_wait(barrier, len(peers))

    def q_own_copy(d):
        to = along_z(d)
        return remote(
            q_send.at[own_head(to)], qb.at[OWN_SLOT[d], pl.ds(0, HD)],
            q_ssem.at[d], q_rsem.at[d], dev(x, to, c),
        )

    def q_shared_copy(i):
        to = along_z(shared_step(i))
        return remote(
            q_send.at[shared_head(to)], qb.at[SHARED_SLOT[i], pl.ds(HD, HD)],
            q_ssem.at[7 + i], q_rsem.at[7 + i], dev(x, to, c),
        )

    def z_copy(d):
        to = along_z(d)
        return remote(kv_send.at[to], kv.at[d, slab], z_ssem.at[d], z_rsem.at[d], dev(x, to, c))

    def sibling_copy(d):
        return remote(kv.at[d, slab], kv.at[d, slab], a_ssem.at[d], a_rsem.at[d], sibling)

    def across_copy(d):
        return remote(kv.at[d, slab], kv.at[d, slab], x_ssem.at[d], x_rsem.at[d], across)

    def second_copy(d):
        there = 2 * (1 - x) + c
        return remote(kv.at[d, there], kv.at[d, there], b_ssem.at[d], b_rsem.at[d], sibling)

    across_copy(0).start()
    sibling_copy(0).start()
    for d in (4, 3, 5, 2, 6, 1, 7):
        q_own_copy(d).start()
        if d <= 3:
            q_shared_copy(d).start()
    for d in (1, 7, 2, 6, 3, 5, 4):
        z_copy(d).start()

    acc_scr[...] = jnp.zeros_like(acc_scr)
    m_scr[...] = jnp.full_like(m_scr, -1e30)
    ones = jnp.ones((16, CHUNK), BF16)

    def chunk_at(t):
        return lax.rem(jnp.where(lax.rem(t, 2) == 1, (t + 1) // 2, Z - t // 2), Z)

    def first_hop(t):
        d = chunk_at(t)
        z_copy(d).wait_recv()
        across_copy(d).start()
        sibling_copy(d).start()

    def second_hop(t):
        d = chunk_at(t)
        across_copy(d).wait_recv()
        second_copy(d).start()

    def arrived(t):
        d = chunk_at(t)
        sibling_copy(d).wait_recv()
        second_copy(d).wait_recv()

    def scores(t, b, slot):
        d = chunk_at(t)
        query = qb[b]
        top = None
        for s in range(4):
            part = jnp.dot(kv[d, s, :ROWS, :], query, preferred_element_type=F32)
            s_scr[slot, s * ROWS : (s + 1) * ROWS, :] = part
            part_top = jnp.max(part.reshape(ROWS // 8, 8, ROWS), axis=0)
            top = part_top if top is None else jnp.maximum(top, part_top)
        mx_scr[slot] = jnp.max(top, axis=0, keepdims=True) * EXP_SCALE

    def weigh(t, b, slot):
        d = chunk_at(t)
        is_shared = (b == SHARED_SLOT[0]) | (b == SHARED_SLOT[1]) | (b == SHARED_SLOT[2]) | (b == SHARED_SLOT[3])
        head_row = pl.multiple_of(jnp.where(is_shared, HD, 0), HD)
        old = m_scr[b]
        new = jnp.maximum(old, mx_scr[slot])
        m_scr[b] = new
        weights, values = [], []
        for s in range(4):
            part = s_scr[slot, s * ROWS : (s + 1) * ROWS, :] * EXP_SCALE - new
            weights.append(jnp.exp2(part).astype(BF16))
            values.append(kv[d, s, pl.ds(ROWS + head_row, HD), :])
            values.append(kv[d, s, pl.ds(ROWS + 128 + head_row, HD), :])
        values = jnp.concatenate([jnp.concatenate(values, axis=1), ones], axis=0)
        product = jnp.dot(values, jnp.concatenate(weights, axis=0), preferred_element_type=F32)
        total = acc_scr[b] * jnp.exp2(old - new) + product
        acc_scr[b] = total
        return total

    second_hop(0)
    first_hop(1)
    for d in range(1, Z):
        q_own_copy(d).wait_recv()
    for i in range(1, 4):
        q_shared_copy(i).wait_recv()
    arrived(0)
    scores(0, 0, 0)

    groups = BLOCKS // UNROLL

    def step(i, carry):
        t, g = i // groups, lax.rem(i, groups)

        @pl.when((g == 0) & (t < Z - 2))
        def _():
            first_hop(t + 2)

        @pl.when(g == 1)
        def _():
            second_hop(t + 1)

        @pl.when(g == 2)
        def _():
            arrived(t + 1)

        for u in range(UNROLL):
            n = i * UNROLL + u
            scores((n + 1) // BLOCKS, lax.rem(n + 1, BLOCKS), (u + 1) % 2)
            weigh(n // BLOCKS, lax.rem(n, BLOCKS), u % 2)
        return carry

    lax.fori_loop(0, (Z - 1) * groups, step, 0)

    def context_copy(b):
        if b in OWN_SLOT:
            d = OWN_SLOT.index(b)
            to, head, sem = along_z(-d), own_head(z), d
        else:
            i = SHARED_SLOT.index(b)
            to, head, sem = along_z(home_step(i)), shared_head(z), 7 + i
        return remote(ctx_send.at[b], ctx_t.at[head], c_ssem.at[sem], c_rsem.at[sem], dev(x, to, c))

    home_slots = (OWN_SLOT[0], SHARED_SLOT[0])
    for b in range(BLOCKS):
        if b + 1 < BLOCKS:
            scores(Z - 1, b + 1, (b + 1) % 2)
        total = weigh(Z - 1, b, b % 2)
        context = (total[:HD] / total[HD : HD + 1]).astype(BF16)
        if b == OWN_SLOT[0]:
            ctx_t[own_head(z)] = context
        elif b == SHARED_SLOT[0]:
            ctx_t[shared_head(z)] = context
        else:
            ctx_send[b] = context
            context_copy(b).start()

    for load in loads:
        load.wait()
    for b in range(BLOCKS):
        if b not in home_slots:
            context_copy(b).wait_recv()

    context = ctx_t[...].reshape(BLOCKS * HD, ROWS).T
    residual = frames[...].astype(F32) + jnp.dot(context, wout[...], preferred_element_type=F32)
    att_ref[...] = residual.astype(BF16)
    centered = residual - jnp.mean(residual, axis=1, keepdims=True)
    variance = jnp.mean(centered * centered, axis=1, keepdims=True)
    normed = (centered * lax.rsqrt(variance + 1e-05) * gain_ref[...]).astype(BF16)
    projected = jnp.dot(normed, wglu[...], preferred_element_type=F32)
    channels = projected.shape[1] // 2
    gated = (projected[:, :channels] * jax.nn.sigmoid(projected[:, channels:])).astype(BF16)

    halo_send[0] = gated[:16]
    halo_send[1] = gated[ROWS - 16 :]
    to_left = remote(halo_send.at[0], halo_recv.at[1], h_ssem.at[0], h_rsem.at[1], left)
    to_right = remote(halo_send.at[1], halo_recv.at[0], h_ssem.at[1], h_rsem.at[0], right)
    to_left.start()
    to_right.start()
    gpad[16 : 16 + ROWS, :] = gated.astype(F32)
    to_left.wait_recv()
    to_right.wait_recv()
    gpad[:16, :] = jnp.where(me == 0, 0.0, halo_recv[0].astype(F32))
    gpad[16 + ROWS :, :] = jnp.where(me == 31, 0.0, halo_recv[1].astype(F32))

    for col in range(0, channels, 128):
        cols = slice(col, col + 128)
        conv = None
        for r in range(8):
            part = None
            for u in range(r, 32, 8):
                if u == 0:
                    continue
                term = gpad[u - r : u - r + ROWS + 8, cols] * dw_ref[u - 1 : u, cols]
                part = term if part is None else part + term
            taps_tmp[r] = part
            shifted = taps_tmp[r, r : r + ROWS, :]
            conv = shifted if conv is None else conv + shifted
        u = bns_ref[:, cols] * conv + bnb_ref[:, cols]
        conv_ref[:, cols] = (u * jax.nn.sigmoid(u)).astype(BF16)

    for d in range(Z):
        if d:
            q_own_copy(d).wait_send()
            z_copy(d).wait_send()
        across_copy(d).wait_send()
        sibling_copy(d).wait_send()
        second_copy(d).wait_send()
    for i in range(1, 4):
        q_shared_copy(i).wait_send()
    for b in range(BLOCKS):
        if b not in home_slots:
            context_copy(b).wait_send()
    to_left.wait_send()
    to_right.wait_send()


def local(frames_in, queries, keys, values, w_out, ln_gain, w_glu, dw_weight, bn_scale, bn_shift):
    rows, width = frames_in.shape
    channels = w_glu.shape[1] // 2
    vmem, hbm = pl.BlockSpec(memory_space=pltpu.VMEM), pl.BlockSpec(memory_space=pl.ANY)
    sems = [pltpu.SemaphoreType.DMA((n,)) for n in (3, 11, 11, Z, Z, Z, Z, Z, Z, Z, Z, 11, 11, 2, 2)]
    return pl.pallas_call(
        kernel,
        out_shape=(
            jax.ShapeDtypeStruct((rows, width), BF16),
            jax.ShapeDtypeStruct((rows, channels), BF16),
        ),
        in_specs=[hbm, vmem, vmem, vmem, hbm, vmem, hbm, vmem, vmem, vmem],
        out_specs=(vmem, vmem),
        scratch_shapes=[
            pltpu.VMEM((Z, 2 * ROWS, 128), BF16),
            pltpu.VMEM((BLOCKS, HD, ROWS), BF16),
            pltpu.VMEM((Z, 4, 2 * ROWS, 128), BF16),
            pltpu.VMEM((BLOCKS, 2 * HD, ROWS), BF16),
            pltpu.VMEM((BLOCKS, HD, ROWS), BF16),
            pltpu.VMEM((BLOCKS, HD, ROWS), BF16),
            pltpu.VMEM((2, CHUNK, ROWS), F32),
            pltpu.VMEM((2, 1, ROWS), F32),
            pltpu.VMEM((BLOCKS, 1, ROWS), F32),
            pltpu.VMEM((BLOCKS, HD + 16, ROWS), F32),
            pltpu.VMEM((rows, width), BF16),
            pltpu.VMEM(w_out.shape, BF16),
            pltpu.VMEM(w_glu.shape, BF16),
            pltpu.VMEM((ROWS + 32, channels), F32),
            pltpu.VMEM((8, ROWS + 8, 128), F32),
            pltpu.VMEM((2, 16, channels), BF16),
            pltpu.VMEM((2, 16, channels), BF16),
        ]
        + sems,
        compiler_params=pltpu.CompilerParams(
            collective_id=0, has_side_effects=True, vmem_limit_bytes=56 * 2**20
        ),
    )(
        frames_in, queries, keys, values, w_out, ln_gain.reshape(1, -1), w_glu, dw_weight,
        bn_scale.reshape(1, -1), bn_shift.reshape(1, -1),
    )


def solution(mesh):
    split = P(("dp", "seq"), None)
    return jax.shard_map(
        local,
        mesh=mesh,
        in_specs=(split,) * 4 + (P(),) * 6,
        out_specs=(split, split),
        check_vma=False,
    )
```

```python
import jax
import jax.numpy as jnp
from jax import lax
from jax.experimental import pallas as pl
from jax.experimental.pallas import tpu as pltpu
from jax.sharding import PartitionSpec as P

MESH = pl.DeviceIdType.MESH
BF16 = jnp.bfloat16
F32 = jnp.float32

HD = 64
TAPS = 31
ROWS = 256
Z = 8
HALF = ROWS // 2
CHUNK = 1024
EXP_SCALE = 0.125 * 1.4426950408889634
OWN_HEADS = (0, 2, 3, 5, 6, 8, 9, 11)
SHARED_HEADS = (1, 4, 7, 10)
EDGE = 16

STEPS = (0, 1, 7, 2, 6, 3, 5, 4)
OWN, SHARED = 0, 1


def kernel(
    frames_hbm, q_ref, k_ref, v_ref, wout_hbm, gain_ref, wglu_hbm, dw_ref, bns_ref, bnb_ref,
    att_ref, conv_ref,
    kv_send, q_send, kv, qb, ctx_send, ctx_t, s_scr, mx_scr, m_scr, acc_scr,
    frames, wout, wglu, gpad, taps_tmp, halo_send, halo_recv,
    local_sem, q_ssem, q_rsem, z_ssem, z_rsem, a_ssem, a_rsem, x_ssem, x_rsem, b_ssem, b_rsem,
    p_ssem, p_rsem, c_ssem, c_rsem, h_ssem, h_rsem,
):
    me = lax.axis_index("seq")
    x, z, c = me // 16, lax.rem(me // 2, Z), lax.rem(me, 2)
    odd = lax.rem(z, 2)
    slab, slab_across = 2 * x + c, 2 * (1 - x) + c

    def dev(x, z, c):
        return {"seq": (x * Z + z) * 2 + c}

    def along_z(step):
        return lax.rem(z + step + Z, Z)

    sibling = dev(x, z, 1 - c)
    across = dev(1 - x, z, c)
    partner = dev(x, z + 1 - 2 * odd, c)
    left = {"seq": lax.rem(me + 31, 32)}
    right = {"seq": lax.rem(me + 1, 32)}
    other = {"seq": jnp.where(c == 1, lax.rem(me + 1, 32), lax.rem(me + 31, 32))}

    def remote(src, dst, ssem, rsem, to):
        return pltpu.make_async_remote_copy(
            src_ref=src, dst_ref=dst, send_sem=ssem, recv_sem=rsem, device_id=to, device_id_type=MESH
        )

    barrier = pltpu.get_barrier_semaphore()
    peers = [dev(x, along_z(d), c) for d in range(1, Z)] + [sibling, across, other]
    for peer in peers:
        pl.semaphore_signal(barrier, inc=1, device_id=peer, device_id_type=MESH)

    loads = [
        pltpu.make_async_copy(frames_hbm, frames, local_sem.at[0]),
        pltpu.make_async_copy(wout_hbm, wout, local_sem.at[1]),
        pltpu.make_async_copy(wglu_hbm, wglu, local_sem.at[2]),
    ]
    for load in loads:
        load.start()

    q_send[...] = q_ref[...].T.reshape(q_send.shape)
    v_t = v_ref[...].T
    for head in range(12):
        cols = slice(head * HD, (head + 1) * HD)
        kv_send[head, :HALF, :] = jnp.concatenate([k_ref[:HALF, cols], k_ref[HALF:, cols]], axis=1)
        kv_send[head, HALF : HALF + HD, :] = v_t[cols, :HALF]
        kv_send[head, HALF + HD :, :] = v_t[cols, HALF:]

    def own_head(zz):
        return 3 * (zz // 2) + 2 * lax.rem(zz, 2)

    def shared_head(zz):
        return 3 * (zz // 2) + 1

    def shared_step(i):
        return jnp.where(lax.rem(z + i, 2) == 0, i, -i)

    def home_step(i):
        return jnp.where(odd == 1, i, -i)

    qb[0] = q_send[own_head(z)]
    qb[8] = q_send[shared_head(z)]
    kv[OWN, 0, slab] = kv_send[own_head(z)]
    kv[SHARED, 0, slab] = kv_send[shared_head(z)]

    pl.semaphore_wait(barrier, len(peers))

    def q_own_copy(n):
        to = along_z(STEPS[n])
        return remote(q_send.at[own_head(to)], qb.at[n], q_ssem.at[n], q_rsem.at[n], dev(x, to, c))

    def q_shared_copy(i):
        to = along_z(shared_step(i))
        return remote(
            q_send.at[shared_head(to)], qb.at[8 + i], q_ssem.at[8 + i], q_rsem.at[8 + i], dev(x, to, c)
        )

    def own_z_copy(n, step):
        to = along_z(step)
        return remote(
            kv_send.at[own_head(to)], kv.at[OWN, n, slab], z_ssem.at[OWN, n], z_rsem.at[OWN, n], dev(x, to, c)
        )

    def shared_z_copy(i):
        to = along_z(shared_step(i))
        return remote(
            kv_send.at[shared_head(to)], kv.at[SHARED, 2 * i, slab],
            z_ssem.at[SHARED, i], z_rsem.at[SHARED, i], dev(x, to, c),
        )

    def partner_copy(i):
        return remote(
            kv.at[SHARED, 2 * i, slab], kv.at[SHARED, 2 * i + 1, slab], p_ssem.at[i], p_rsem.at[i], partner
        )

    def sibling_copy(h, n):
        part = kv.at[h, n, slab]
        return remote(part, part, a_ssem.at[h, n], a_rsem.at[h, n], sibling)

    def across_copy(h, n):
        part = kv.at[h, n, slab]
        return remote(part, part, x_ssem.at[h, n], x_rsem.at[h, n], across)

    def second_copy(h, n):
        part = kv.at[h, n, slab_across]
        return remote(part, part, b_ssem.at[h, n], b_rsem.at[h, n], sibling)

    def spread(h, n):
        across_copy(h, n).start()
        sibling_copy(h, n).start()

    def own_first(n):
        own_z_copy(n, 0).wait_recv()
        spread(OWN, n)

    def shared_first(n):
        if n % 2 == 0:
            shared_z_copy(n // 2).wait_recv()
            partner_copy(n // 2).start()
        else:
            partner_copy(n // 2).wait_recv()
        spread(SHARED, n)

    def second(h, n):
        across_copy(h, n).wait_recv()
        second_copy(h, n).start()

    def arrived(h, n):
        sibling_copy(h, n).wait_recv()
        second_copy(h, n).wait_recv()

    spread(OWN, 0)
    for n in (1, 2):
        own_z_copy(n, STEPS[n]).start()
    for n in range(1, Z):
        q_own_copy(n).start()
    spread(SHARED, 0)
    partner_copy(0).start()
    for i in range(1, 4):
        q_shared_copy(i).start()
    for n in range(3, Z):
        own_z_copy(n, STEPS[n]).start()
    for i in range(1, 4):
        shared_z_copy(i).start()

    acc_scr[...] = jnp.zeros_like(acc_scr)
    m_scr[...] = jnp.full_like(m_scr, -1e30)
    ones = jnp.ones((16, CHUNK), BF16)
    zeros = jnp.zeros((HD, ROWS), BF16)

    def scores(h, n, b, slot):
        query = qb[b]
        keys = jnp.concatenate([kv[h, n, s, :HALF, :] for s in range(4)], axis=0)
        top = None
        for half in range(2):
            weight = jnp.concatenate([query, zeros] if half == 0 else [zeros, query], axis=0)
            part = jnp.dot(keys, weight, preferred_element_type=F32)
            s_scr[slot, half * 4 * HALF : (half + 1) * 4 * HALF, :] = part
            part_top = jnp.max(part.reshape(HALF // 2, 8, ROWS), axis=0)
            top = part_top if top is None else jnp.maximum(top, part_top)
        mx_scr[slot] = jnp.max(top, axis=0, keepdims=True) * EXP_SCALE

    def weigh(h, n, b, slot):
        old = m_scr[b]
        new = jnp.maximum(old, mx_scr[slot])
        m_scr[b] = new
        weights, values = [], []
        for half in range(2):
            part = s_scr[slot, half * 4 * HALF : (half + 1) * 4 * HALF, :] * EXP_SCALE - new
            weights.append(jnp.exp2(part).astype(BF16))
            first = HALF + half * HD
            values += [kv[h, n, s, first : first + HD, :] for s in range(4)]
        values = jnp.concatenate([jnp.concatenate(values, axis=1), ones], axis=0)
        product = jnp.dot(values, jnp.concatenate(weights, axis=0), preferred_element_type=F32)
        total = acc_scr[b] * jnp.exp2(old - new) + product
        acc_scr[b] = total
        return total

    def context_copy(b):
        if b < 8:
            to, head = along_z(-STEPS[b]), own_head(z)
        else:
            to, head = along_z(home_step(b - 8)), shared_head(z)
        return remote(ctx_send.at[b], ctx_t.at[head], c_ssem.at[b], c_rsem.at[b], dev(x, to, c))

    def finish(b, total):
        context = (total[:HD] / total[HD : HD + 1]).astype(BF16)
        if b == 0:
            ctx_t[own_head(z)] = context
        elif b == 8:
            ctx_t[shared_head(z)] = context
        else:
            ctx_send[b] = context
            context_copy(b).start()

    def place(r, u):
        if isinstance(r, int):
            if r == 3 or r > 8:
                return SHARED, 2 * (0 if r == 3 else r - 8) + u // 4, 8 + u % 4
            return OWN, r - (r > 3), u
        is_shared = (r == 3) | (r > 8)
        unit = jnp.where(is_shared, 2 * jnp.where(r == 3, 0, r - 8) + u // 4, r - jnp.where(r > 3, 1, 0))
        return jnp.where(is_shared, SHARED, OWN), unit, jnp.where(is_shared, 8 + u % 4, u)

    plan = {
        (1, 4): lambda: second(SHARED, 1),
        (1, 7): lambda: arrived(OWN, 2),
        (2, 0): lambda: own_first(3),
        (2, 4): lambda: own_first(4),
        (2, 7): lambda: (arrived(SHARED, 0), arrived(SHARED, 1), [q_shared_copy(i).wait_recv() for i in (1, 2, 3)]),
        (3, 0): lambda: second(OWN, 3),
        (3, 4): lambda: second(OWN, 4),
        (3, 7): lambda: arrived(OWN, 3),
        (4, 0): lambda: own_first(5),
        (4, 4): lambda: own_first(6),
        (4, 7): lambda: arrived(OWN, 4),
        (5, 0): lambda: second(OWN, 5),
        (5, 4): lambda: (second(OWN, 6), own_first(7)),
        (5, 7): lambda: arrived(OWN, 5),
        (6, 0): lambda: shared_first(2),
        (6, 4): lambda: second(OWN, 7),
        (6, 7): lambda: arrived(OWN, 6),
        (7, 0): lambda: shared_first(4),
        (7, 4): lambda: (shared_first(6), second(SHARED, 2)),
        (7, 7): lambda: arrived(OWN, 7),
        (9, 0): lambda: second(SHARED, 5),
        (9, 4): lambda: second(SHARED, 7),
        (9, 7): lambda: (arrived(SHARED, 4), arrived(SHARED, 5)),
        (10, 7): lambda: (arrived(SHARED, 6), arrived(SHARED, 7)),
    }

    def pass_on(r, u):
        for (at, step), action in plan.items():
            if step == u:
                pl.when(r == at)(lambda action=action: (action(), None)[1])

    def round_of_eight(r, carry):
        for u in range(8):
            pass_on(r, u)
            scores(*(place(r, u + 1) if u < 7 else place(r + 1, 0)), (u + 1) % 2)
            weigh(*place(r, u), u % 2)
        return carry

    second(OWN, 0)
    arrived(OWN, 0)
    scores(OWN, 0, 0, 0)
    for u in range(8):
        if u == 2:
            own_first(1)
            own_first(2)
        if u == 4:
            second(SHARED, 0)
            shared_first(1)
        if u == 6:
            second(OWN, 1)
            second(OWN, 2)
        if u < 7:
            q_own_copy(u + 1).wait_recv()
            scores(OWN, 0, u + 1, (u + 1) % 2)
        else:
            arrived(OWN, 1)
            scores(OWN, 1, 0, 0)
        weigh(OWN, 0, u, u % 2)

    lax.fori_loop(1, 8, round_of_eight, 0)

    order = (0, 7, 6, 5, 4, 3, 2, 1)
    for u, b in enumerate(order):
        if u == 0:
            shared_first(3)
        if u == 2:
            second(SHARED, 4)
        if u == 4:
            shared_first(5)
            second(SHARED, 6)
        if u == 6:
            shared_first(7)
            second(SHARED, 3)
        if u < 7:
            scores(OWN, 7, order[u + 1], (u + 1) % 2)
        else:
            arrived(SHARED, 2)
            arrived(SHARED, 3)
            scores(SHARED, 2, 8, 0)
        finish(b, weigh(OWN, 7, b, u % 2))

    lax.fori_loop(9, 11, round_of_eight, 0)

    for u in range(8):
        if u < 7:
            scores(*place(11, u + 1), (u + 1) % 2)
        total = weigh(*place(11, u), u % 2)
        if u >= 4:
            finish(4 + u, total)

    for load in loads:
        load.wait()

    def project(heads):
        context = jnp.concatenate([ctx_t[h] for h in heads], axis=0).T
        weight = jnp.concatenate([wout[h * HD : (h + 1) * HD, :] for h in heads], axis=0)
        return jnp.dot(context, weight, preferred_element_type=F32)

    for b in range(1, 8):
        context_copy(b).wait_recv()
    residual = frames[...].astype(F32) + project(OWN_HEADS)
    for b in range(9, 12):
        context_copy(b).wait_recv()
    residual = residual + project(SHARED_HEADS)
    att_ref[...] = residual.astype(BF16)
    centered = residual - jnp.mean(residual, axis=1, keepdims=True)
    variance = jnp.mean(centered * centered, axis=1, keepdims=True)
    gain = gain_ref[...].reshape(1, -1)
    normed = (centered * lax.rsqrt(variance + 1e-05) * gain).astype(BF16)
    projected = jnp.dot(normed, wglu[...], preferred_element_type=F32)
    channels = projected.shape[1] // 2
    gated = (projected[:, :channels] * jax.nn.sigmoid(projected[:, channels:])).astype(BF16)

    halo_send[0] = gated[:EDGE]
    halo_send[1] = gated[ROWS - EDGE :]
    to_left = remote(halo_send.at[0], halo_recv.at[1], h_ssem.at[0], h_rsem.at[1], left)
    to_right = remote(halo_send.at[1], halo_recv.at[0], h_ssem.at[1], h_rsem.at[0], right)
    to_left.start()
    to_right.start()
    gpad[EDGE : EDGE + ROWS, :] = gated.astype(F32)
    bn_scale, bn_shift = bns_ref[...].reshape(1, -1), bnb_ref[...].reshape(1, -1)

    def convolve(first, rows):
        for col in range(0, channels, 128):
            cols = slice(col, col + 128)
            conv = None
            for r in range(8):
                part = None
                for u in range(r, 32, 8):
                    if u == 0:
                        continue
                    begin = first + u - r
                    term = gpad[begin : begin + rows + 8, cols] * dw_ref[u - 1 : u, cols]
                    part = term if part is None else part + term
                taps_tmp[r, : rows + 8] = part
                shifted = taps_tmp[r, r : r + rows, :]
                conv = shifted if conv is None else conv + shifted
            u = bn_scale[:, cols] * conv + bn_shift[:, cols]
            conv_ref[first : first + rows, cols] = (u * jax.nn.sigmoid(u)).astype(BF16)

    convolve(EDGE, ROWS - 2 * EDGE)
    to_left.wait_recv()
    to_right.wait_recv()
    gpad[:EDGE, :] = jnp.where(me == 0, 0.0, halo_recv[0].astype(F32))
    gpad[EDGE + ROWS :, :] = jnp.where(me == 31, 0.0, halo_recv[1].astype(F32))
    convolve(0, EDGE)
    convolve(ROWS - EDGE, EDGE)

    for n in range(1, Z):
        q_own_copy(n).wait_send()
        own_z_copy(n, STEPS[n]).wait_send()
    for i in range(1, 4):
        q_shared_copy(i).wait_send()
        shared_z_copy(i).wait_send()
    for i in range(4):
        partner_copy(i).wait_send()
    for h in (OWN, SHARED):
        for n in range(Z):
            across_copy(h, n).wait_send()
            sibling_copy(h, n).wait_send()
            second_copy(h, n).wait_send()
    for b in range(12):
        if b not in (0, 8):
            context_copy(b).wait_send()
    to_left.wait_send()
    to_right.wait_send()


def hand_on(att_in, conv_in, att_out, conv_out):
    att_out[...] = att_in[...]
    conv_out[...] = conv_in[...]


def local(frames_in, queries, keys, values, w_out, ln_gain, w_glu, dw_weight, bn_scale, bn_shift):
    rows, width = frames_in.shape
    channels = w_glu.shape[1] // 2
    vmem, hbm = pl.BlockSpec(memory_space=pltpu.VMEM), pl.BlockSpec(memory_space=pl.ANY)
    dma = pltpu.SemaphoreType.DMA
    units = [dma((2, Z))] * 8
    out_shape = (
        jax.ShapeDtypeStruct((rows, width), BF16),
        jax.ShapeDtypeStruct((rows, channels), BF16),
    )
    results = pl.pallas_call(
        kernel,
        out_shape=out_shape,
        in_specs=[hbm, vmem, vmem, vmem, hbm, vmem, hbm, vmem, vmem, vmem],
        out_specs=(vmem, vmem),
        scratch_shapes=[
            pltpu.VMEM((12, ROWS, 128), BF16),
            pltpu.VMEM((12, HD, ROWS), BF16),
            pltpu.VMEM((2, Z, 4, ROWS, 128), BF16),
            pltpu.VMEM((12, HD, ROWS), BF16),
            pltpu.VMEM((12, HD, ROWS), BF16),
            pltpu.VMEM((12, HD, ROWS), BF16),
            pltpu.VMEM((2, CHUNK, ROWS), F32),
            pltpu.VMEM((2, 1, ROWS), F32),
            pltpu.VMEM((12, 1, ROWS), F32),
            pltpu.VMEM((12, HD + 16, ROWS), F32),
            pltpu.VMEM((rows, width), BF16),
            pltpu.VMEM(w_out.shape, BF16),
            pltpu.VMEM(w_glu.shape, BF16),
            pltpu.VMEM((ROWS + 2 * EDGE, channels), F32),
            pltpu.VMEM((8, ROWS + 8, 128), F32),
            pltpu.VMEM((2, EDGE, channels), BF16),
            pltpu.VMEM((2, EDGE, channels), BF16),
            dma((3,)),
            dma((12,)),
            dma((12,)),
        ]
        + units
        + [dma((4,)), dma((4,)), dma((12,)), dma((12,)), dma((2,)), dma((2,))],
        compiler_params=pltpu.CompilerParams(
            collective_id=0, has_side_effects=True, vmem_limit_bytes=56 * 2**20
        ),
    )(frames_in, queries, keys, values, w_out, ln_gain, w_glu, dw_weight, bn_scale, bn_shift)
    return pl.pallas_call(
        hand_on,
        out_shape=out_shape,
        in_specs=[vmem, vmem],
        out_specs=(vmem, vmem),
    )(*results)


def solution(mesh):
    split = P(("dp", "seq"), None)
    return jax.shard_map(
        local,
        mesh=mesh,
        in_specs=(split,) * 4 + (P(),) * 6,
        out_specs=(split, split),
        check_vma=False,
    )
```

```python
import jax
import jax.numpy as jnp
from jax import lax
from jax.experimental import pallas as pl
from jax.experimental.pallas import tpu as pltpu
from jax.sharding import PartitionSpec as P

MESH = pl.DeviceIdType.MESH
BF16 = jnp.bfloat16
F32 = jnp.float32

HD = 64
TAPS = 31
ROWS = 256
Z = 8
HALF = ROWS // 2
CHUNK = 1024
EXP_SCALE = 0.125 * 1.4426950408889634
OWN_HEADS = (0, 2, 3, 5, 6, 8, 9, 11)
SHARED_HEADS = (1, 4, 7, 10)
EDGE = 16

STEPS = (0, 1, 7, 2, 6, 3, 5, 4)
OWN, SHARED = 0, 1


def kernel(
    frames_hbm, q_ref, k_ref, v_ref, wout_hbm, gain_ref, wglu_hbm, dw_ref, bns_ref, bnb_ref,
    att_ref, conv_ref,
    kv_send, q_send, kv, qb, ctx_send, ctx_t, s_scr, mx_scr, m_scr, acc_scr,
    frames, wout, wglu, gpad, taps_tmp, halo_send, halo_recv,
    local_sem, q_ssem, q_rsem, z_ssem, z_rsem, a_ssem, a_rsem, x_ssem, x_rsem, b_ssem, b_rsem,
    p_ssem, p_rsem, c_ssem, c_rsem, h_ssem, h_rsem,
):
    me = lax.axis_index("seq")
    x, z, c = me // 16, lax.rem(me // 2, Z), lax.rem(me, 2)
    odd = lax.rem(z, 2)
    slab, slab_across = 2 * x + c, 2 * (1 - x) + c

    def dev(x, z, c):
        return {"seq": (x * Z + z) * 2 + c}

    def along_z(step):
        return lax.rem(z + step + Z, Z)

    sibling = dev(x, z, 1 - c)
    across = dev(1 - x, z, c)
    partner = dev(x, z + 1 - 2 * odd, c)
    left = {"seq": lax.rem(me + 31, 32)}
    right = {"seq": lax.rem(me + 1, 32)}
    other = {"seq": jnp.where(c == 1, lax.rem(me + 1, 32), lax.rem(me + 31, 32))}

    def remote(src, dst, ssem, rsem, to):
        return pltpu.make_async_remote_copy(
            src_ref=src, dst_ref=dst, send_sem=ssem, recv_sem=rsem, device_id=to, device_id_type=MESH
        )

    barrier = pltpu.get_barrier_semaphore()
    peers = [dev(x, along_z(d), c) for d in range(1, Z)] + [sibling, across, other]
    for peer in peers:
        pl.semaphore_signal(barrier, inc=1, device_id=peer, device_id_type=MESH)

    loads = [
        pltpu.make_async_copy(frames_hbm, frames, local_sem.at[0]),
        pltpu.make_async_copy(wout_hbm, wout, local_sem.at[1]),
        pltpu.make_async_copy(wglu_hbm, wglu, local_sem.at[2]),
    ]
    for load in loads:
        load.start()

    q_send[...] = q_ref[...].T.reshape(q_send.shape)
    v_t = v_ref[...].T
    for head in range(12):
        cols = slice(head * HD, (head + 1) * HD)
        kv_send[head, :HALF, :] = jnp.concatenate([k_ref[:HALF, cols], k_ref[HALF:, cols]], axis=1)
        kv_send[head, HALF : HALF + HD, :] = v_t[cols, :HALF]
        kv_send[head, HALF + HD :, :] = v_t[cols, HALF:]

    def own_head(zz):
        return 3 * (zz // 2) + 2 * lax.rem(zz, 2)

    def shared_head(zz):
        return 3 * (zz // 2) + 1

    def shared_step(i):
        return jnp.where(lax.rem(z + i, 2) == 0, i, -i)

    def home_step(i):
        return jnp.where(odd == 1, i, -i)

    qb[0] = q_send[own_head(z)]
    qb[8] = q_send[shared_head(z)]
    kv[OWN, 0, slab] = kv_send[own_head(z)]
    kv[SHARED, 0, slab] = kv_send[shared_head(z)]

    pl.semaphore_wait(barrier, len(peers))

    def q_own_copy(n):
        to = along_z(STEPS[n])
        return remote(q_send.at[own_head(to)], qb.at[n], q_ssem.at[n], q_rsem.at[n], dev(x, to, c))

    def q_shared_copy(i):
        to = along_z(shared_step(i))
        return remote(
            q_send.at[shared_head(to)], qb.at[8 + i], q_ssem.at[8 + i], q_rsem.at[8 + i], dev(x, to, c)
        )

    def own_z_copy(n, step):
        to = along_z(step)
        return remote(
            kv_send.at[own_head(to)], kv.at[OWN, n, slab], z_ssem.at[OWN, n], z_rsem.at[OWN, n], dev(x, to, c)
        )

    def shared_z_copy(i):
        to = along_z(shared_step(i))
        return remote(
            kv_send.at[shared_head(to)], kv.at[SHARED, 2 * i, slab],
            z_ssem.at[SHARED, i], z_rsem.at[SHARED, i], dev(x, to, c),
        )

    def partner_copy(i):
        return remote(
            kv.at[SHARED, 2 * i, slab], kv.at[SHARED, 2 * i + 1, slab], p_ssem.at[i], p_rsem.at[i], partner
        )

    def sibling_copy(h, n):
        part = kv.at[h, n, slab]
        return remote(part, part, a_ssem.at[h, n], a_rsem.at[h, n], sibling)

    def across_copy(h, n):
        part = kv.at[h, n, slab]
        return remote(part, part, x_ssem.at[h, n], x_rsem.at[h, n], across)

    def second_copy(h, n):
        part = kv.at[h, n, slab_across]
        return remote(part, part, b_ssem.at[h, n], b_rsem.at[h, n], sibling)

    def spread(h, n):
        across_copy(h, n).start()
        sibling_copy(h, n).start()

    def own_first(n):
        own_z_copy(n, 0).wait_recv()
        spread(OWN, n)

    def shared_first(n):
        if n % 2 == 0:
            shared_z_copy(n // 2).wait_recv()
            partner_copy(n // 2).start()
        else:
            partner_copy(n // 2).wait_recv()
        spread(SHARED, n)

    def second(h, n):
        across_copy(h, n).wait_recv()
        second_copy(h, n).start()

    def arrived(h, n):
        sibling_copy(h, n).wait_recv()
        second_copy(h, n).wait_recv()

    spread(OWN, 0)
    for n in (1, 2):
        own_z_copy(n, STEPS[n]).start()
    for n in range(1, Z):
        q_own_copy(n).start()
    spread(SHARED, 0)
    partner_copy(0).start()
    for n in (3, 4):
        own_z_copy(n, STEPS[n]).start()
    for i in range(1, 4):
        q_shared_copy(i).start()
    for n in (5, 6, 7):
        own_z_copy(n, STEPS[n]).start()

    acc_scr[...] = jnp.zeros_like(acc_scr)
    m_scr[...] = jnp.full_like(m_scr, -1e30)
    ones = jnp.ones((16, CHUNK), BF16)
    zeros = jnp.zeros((HD, ROWS), BF16)

    def scores(h, n, b, slot):
        query = qb[b]
        keys = jnp.concatenate([kv[h, n, s, :HALF, :] for s in range(4)], axis=0)
        top = None
        for half in range(2):
            weight = jnp.concatenate([query, zeros] if half == 0 else [zeros, query], axis=0)
            part = jnp.dot(keys, weight, preferred_element_type=F32)
            s_scr[slot, half * 4 * HALF : (half + 1) * 4 * HALF, :] = part
            part_top = jnp.max(part.reshape(HALF // 2, 8, ROWS), axis=0)
            top = part_top if top is None else jnp.maximum(top, part_top)
        mx_scr[slot] = jnp.max(top, axis=0, keepdims=True) * EXP_SCALE

    def weigh(h, n, b, slot):
        old = m_scr[b]
        new = jnp.maximum(old, mx_scr[slot])
        m_scr[b] = new
        weights, values = [], []
        for half in range(2):
            part = s_scr[slot, half * 4 * HALF : (half + 1) * 4 * HALF, :] * EXP_SCALE - new
            weights.append(jnp.exp2(part).astype(BF16))
            first = HALF + half * HD
            values += [kv[h, n, s, first : first + HD, :] for s in range(4)]
        values = jnp.concatenate([jnp.concatenate(values, axis=1), ones], axis=0)
        product = jnp.dot(values, jnp.concatenate(weights, axis=0), preferred_element_type=F32)
        total = acc_scr[b] * jnp.exp2(old - new) + product
        acc_scr[b] = total
        return total

    def context_copy(b):
        if b < 8:
            to, head = along_z(-STEPS[b]), own_head(z)
        else:
            to, head = along_z(home_step(b - 8)), shared_head(z)
        return remote(ctx_send.at[b], ctx_t.at[head], c_ssem.at[b], c_rsem.at[b], dev(x, to, c))

    def finish(b, total):
        context = (total[:HD] / total[HD : HD + 1]).astype(BF16)
        if b == 0:
            ctx_t[own_head(z)] = context
        elif b == 8:
            ctx_t[shared_head(z)] = context
        else:
            ctx_send[b] = context
            context_copy(b).start()

    shared_units = {3: (0, 1), 9: (2, 4), 10: (6, 3), 11: (5, 7)}

    def place(r, u):
        if isinstance(r, int):
            if r in shared_units:
                return SHARED, shared_units[r][u // 4], 11 - u % 4
            return OWN, r - (r > 3), 7 - u if r == 8 else u
        unit = jnp.where(r == 3, shared_units[3][u // 4], r - jnp.where(r > 3, 1, 0))
        return jnp.where(r == 3, SHARED, OWN), unit, jnp.where(r == 3, 11 - u % 4, u)

    def each(*actions):
        def run():
            for action, *arguments in actions:
                action(*arguments)

        return run

    def q_arrived(*ids):
        for i in ids:
            if i < 8:
                q_own_copy(i).wait_recv()
            else:
                q_shared_copy(i - 8).wait_recv()

    def send_shared():
        for i in range(1, 4):
            shared_z_copy(i).start()

    plan = {
        (0, 0): each((second, OWN, 0), (own_first, 1), (own_first, 2), (arrived, OWN, 0)),
        (0, 1): each((q_arrived, 1, 2)),
        (0, 3): each((q_arrived, 3, 4)),
        (0, 5): each(
            (q_arrived, 5, 6, 7), (second, OWN, 1), (second, OWN, 2), (second, SHARED, 0), (shared_first, 1)
        ),
        (1, 0): each((send_shared,), (arrived, OWN, 1)),
        (2, 0): each((arrived, OWN, 2), (second, SHARED, 1), (own_first, 3)),
        (3, 0): each((own_first, 4), (q_arrived, 9, 10, 11), (arrived, SHARED, 0), (arrived, SHARED, 1)),
        (4, 0): each((second, OWN, 3), (second, OWN, 4), (own_first, 5), (arrived, OWN, 3)),
        (5, 0): each((own_first, 6), (own_first, 7), (arrived, OWN, 4)),
        (6, 0): each((second, OWN, 5), (second, OWN, 6), (shared_first, 2), (arrived, OWN, 5)),
        (7, 0): each((second, OWN, 7), (shared_first, 4), (shared_first, 6), (arrived, OWN, 6)),
        (8, 0): each((second, SHARED, 2), (arrived, OWN, 7)),
        (8, 4): each((shared_first, 3), (shared_first, 5), (second, SHARED, 4)),
        (9, 0): each((second, SHARED, 6), (shared_first, 7), (arrived, SHARED, 2), (arrived, SHARED, 4)),
        (10, 0): each((second, SHARED, 3), (arrived, SHARED, 6)),
        (10, 4): each((second, SHARED, 5), (arrived, SHARED, 3)),
        (11, 0): each((second, SHARED, 7), (arrived, SHARED, 5)),
        (11, 4): each((arrived, SHARED, 7)),
    }

    def steps(r, before):
        for u in range(8):
            if isinstance(r, int):
                if (r, u) in plan:
                    plan[r, u]()
            elif u == 0:
                for at in range(1, 8):
                    pl.when(r == at)(plan[at, 0])
            scores(*place(r, u), u % 2)
            if u > 0 or before is not None:
                previous = place(r, u - 1) if u else place(before, 7)
                weighed(r if u else before, u - 1 if u else 7, weigh(*previous, (u + 1) % 2))

    def weighed(r, u, total):
        if isinstance(r, int) and (r == 8 or (r == 11 and u >= 4)):
            finish(place(r, u)[2], total)

    steps(0, None)

    def one_round(r, carry):
        steps(r, r - 1)
        return carry

    lax.fori_loop(1, 8, one_round, 0)
    for r in (8, 9, 10, 11):
        steps(r, r - 1)
    weighed(11, 7, weigh(*place(11, 7), 1))

    for load in loads:
        load.wait()

    def project(heads):
        context = jnp.concatenate([ctx_t[h] for h in heads], axis=0).T
        weight = jnp.concatenate([wout[h * HD : (h + 1) * HD, :] for h in heads], axis=0)
        return jnp.dot(context, weight, preferred_element_type=F32)

    for b in range(1, 8):
        context_copy(b).wait_recv()
    residual = frames[...].astype(F32) + project(OWN_HEADS)
    for b in range(9, 12):
        context_copy(b).wait_recv()
    residual = residual + project(SHARED_HEADS)
    att_ref[...] = residual.astype(BF16)
    centered = residual - jnp.mean(residual, axis=1, keepdims=True)
    variance = jnp.mean(centered * centered, axis=1, keepdims=True)
    gain = gain_ref[...].reshape(1, -1)
    normed = (centered * lax.rsqrt(variance + 1e-05) * gain).astype(BF16)
    projected = jnp.dot(normed, wglu[...], preferred_element_type=F32)
    channels = projected.shape[1] // 2
    gated = (projected[:, :channels] * jax.nn.sigmoid(projected[:, channels:])).astype(BF16)

    halo_send[0] = gated[:EDGE]
    halo_send[1] = gated[ROWS - EDGE :]
    to_left = remote(halo_send.at[0], halo_recv.at[1], h_ssem.at[0], h_rsem.at[1], left)
    to_right = remote(halo_send.at[1], halo_recv.at[0], h_ssem.at[1], h_rsem.at[0], right)
    to_left.start()
    to_right.start()
    gpad[EDGE : EDGE + ROWS, :] = gated.astype(F32)
    bn_scale, bn_shift = bns_ref[...].reshape(1, -1), bnb_ref[...].reshape(1, -1)

    def convolve(first, rows):
        for col in range(0, channels, 128):
            cols = slice(col, col + 128)
            conv = None
            for r in range(8):
                part = None
                for u in range(r, 32, 8):
                    if u == 0:
                        continue
                    begin = first + u - r
                    term = gpad[begin : begin + rows + 8, cols] * dw_ref[u - 1 : u, cols]
                    part = term if part is None else part + term
                taps_tmp[r, : rows + 8] = part
                shifted = taps_tmp[r, r : r + rows, :]
                conv = shifted if conv is None else conv + shifted
            u = bn_scale[:, cols] * conv + bn_shift[:, cols]
            conv_ref[first : first + rows, cols] = (u * jax.nn.sigmoid(u)).astype(BF16)

    convolve(EDGE, ROWS - 2 * EDGE)
    to_left.wait_recv()
    to_right.wait_recv()
    gpad[:EDGE, :] = jnp.where(me == 0, 0.0, halo_recv[0].astype(F32))
    gpad[EDGE + ROWS :, :] = jnp.where(me == 31, 0.0, halo_recv[1].astype(F32))
    convolve(0, EDGE)
    convolve(ROWS - EDGE, EDGE)

    for n in range(1, Z):
        q_own_copy(n).wait_send()
        own_z_copy(n, STEPS[n]).wait_send()
    for i in range(1, 4):
        q_shared_copy(i).wait_send()
        shared_z_copy(i).wait_send()
    for i in range(4):
        partner_copy(i).wait_send()
    for h in (OWN, SHARED):
        for n in range(Z):
            across_copy(h, n).wait_send()
            sibling_copy(h, n).wait_send()
            second_copy(h, n).wait_send()
    for b in range(12):
        if b not in (0, 8):
            context_copy(b).wait_send()
    to_left.wait_send()
    to_right.wait_send()


def hand_on(att_in, conv_in, att_out, conv_out):
    att_out[...] = att_in[...]
    conv_out[...] = conv_in[...]


def local(frames_in, queries, keys, values, w_out, ln_gain, w_glu, dw_weight, bn_scale, bn_shift):
    rows, width = frames_in.shape
    channels = w_glu.shape[1] // 2
    vmem, hbm = pl.BlockSpec(memory_space=pltpu.VMEM), pl.BlockSpec(memory_space=pl.ANY)
    dma = pltpu.SemaphoreType.DMA
    units = [dma((2, Z))] * 8
    out_shape = (
        jax.ShapeDtypeStruct((rows, width), BF16),
        jax.ShapeDtypeStruct((rows, channels), BF16),
    )
    results = pl.pallas_call(
        kernel,
        out_shape=out_shape,
        in_specs=[hbm, vmem, vmem, vmem, hbm, vmem, hbm, vmem, vmem, vmem],
        out_specs=(vmem, vmem),
        scratch_shapes=[
            pltpu.VMEM((12, ROWS, 128), BF16),
            pltpu.VMEM((12, HD, ROWS), BF16),
            pltpu.VMEM((2, Z, 4, ROWS, 128), BF16),
            pltpu.VMEM((12, HD, ROWS), BF16),
            pltpu.VMEM((12, HD, ROWS), BF16),
            pltpu.VMEM((12, HD, ROWS), BF16),
            pltpu.VMEM((2, CHUNK, ROWS), F32),
            pltpu.VMEM((2, 1, ROWS), F32),
            pltpu.VMEM((12, 1, ROWS), F32),
            pltpu.VMEM((12, HD + 16, ROWS), F32),
            pltpu.VMEM((rows, width), BF16),
            pltpu.VMEM(w_out.shape, BF16),
            pltpu.VMEM(w_glu.shape, BF16),
            pltpu.VMEM((ROWS + 2 * EDGE, channels), F32),
            pltpu.VMEM((8, ROWS + 8, 128), F32),
            pltpu.VMEM((2, EDGE, channels), BF16),
            pltpu.VMEM((2, EDGE, channels), BF16),
            dma((3,)),
            dma((12,)),
            dma((12,)),
        ]
        + units
        + [dma((4,)), dma((4,)), dma((12,)), dma((12,)), dma((2,)), dma((2,))],
        compiler_params=pltpu.CompilerParams(
            collective_id=0, has_side_effects=True, vmem_limit_bytes=56 * 2**20
        ),
    )(frames_in, queries, keys, values, w_out, ln_gain, w_glu, dw_weight, bn_scale, bn_shift)
    return pl.pallas_call(
        hand_on,
        out_shape=out_shape,
        in_specs=[vmem, vmem],
        out_specs=(vmem, vmem),
    )(*results)


def solution(mesh):
    split = P(("dp", "seq"), None)
    return jax.shard_map(
        local,
        mesh=mesh,
        in_specs=(split,) * 4 + (P(),) * 6,
        out_specs=(split, split),
        check_vma=False,
    )
```

```python
import jax
import jax.numpy as jnp
from jax import lax
from jax.experimental import pallas as pl
from jax.experimental.pallas import tpu as pltpu
from jax.sharding import PartitionSpec as P

MESH = pl.DeviceIdType.MESH
BF16 = jnp.bfloat16
F32 = jnp.float32

HD = 64
TAPS = 31
ROWS = 256
Z = 8
HALF = ROWS // 2
CHUNK = 1024
EXP_SCALE = 0.125 * 1.4426950408889634
OWN_HEADS = (0, 2, 3, 5, 6, 8, 9, 11)
SHARED_HEADS = (1, 4, 7, 10)
EDGE = 16

STEPS = (0, 1, 7, 2, 6, 3, 5, 4)
OWN, SHARED = 0, 1


def kernel(
    frames_hbm, q_hbm, k_hbm, v_hbm, wout_hbm, gain_hbm, wglu_hbm, dw_hbm, bns_hbm, bnb_hbm,
    att_hbm, conv_hbm,
    q_ref, k_ref, v_ref, gain_ref, dw_ref, bns_ref, bnb_ref, att_ref, conv_ref,
    kv_send, q_send, kv, qb, ctx_send, ctx_t, s_scr, mx_scr, m_scr, acc_scr,
    frames, wout, wglu, gpad, taps_tmp, halo_send, halo_recv,
    local_sem, q_ssem, q_rsem, z_ssem, z_rsem, a_ssem, a_rsem, x_ssem, x_rsem, b_ssem, b_rsem,
    p_ssem, p_rsem, c_ssem, c_rsem, h_ssem, h_rsem,
):
    me = lax.axis_index("seq")
    x, z, c = me // 16, lax.rem(me // 2, Z), lax.rem(me, 2)
    odd = lax.rem(z, 2)
    slab, slab_across = 2 * x + c, 2 * (1 - x) + c

    def dev(x, z, c):
        return {"seq": (x * Z + z) * 2 + c}

    def along_z(step):
        return lax.rem(z + step + Z, Z)

    sibling = dev(x, z, 1 - c)
    across = dev(1 - x, z, c)
    partner = dev(x, z + 1 - 2 * odd, c)
    left = {"seq": lax.rem(me + 31, 32)}
    right = {"seq": lax.rem(me + 1, 32)}
    other = {"seq": jnp.where(c == 1, lax.rem(me + 1, 32), lax.rem(me + 31, 32))}

    def remote(src, dst, ssem, rsem, to):
        return pltpu.make_async_remote_copy(
            src_ref=src, dst_ref=dst, send_sem=ssem, recv_sem=rsem, device_id=to, device_id_type=MESH
        )

    barrier = pltpu.get_barrier_semaphore()
    peers = [dev(x, along_z(d), c) for d in range(1, Z)] + [sibling, across, other]
    for peer in peers:
        pl.semaphore_signal(barrier, inc=1, device_id=peer, device_id_type=MESH)

    pairs = [
        (q_hbm, q_ref), (v_hbm, v_ref), (k_hbm, k_ref), (frames_hbm, frames), (wout_hbm, wout), (wglu_hbm, wglu),
        (gain_hbm, gain_ref), (dw_hbm, dw_ref), (bns_hbm, bns_ref), (bnb_hbm, bnb_ref),
    ]
    loads = [pltpu.make_async_copy(src, dst, local_sem.at[i]) for i, (src, dst) in enumerate(pairs)]
    for load in loads:
        load.start()
    for load in loads[:3]:
        load.wait()

    q_send[...] = q_ref[...].T.reshape(q_send.shape)
    v_t = v_ref[...].T
    for head in range(12):
        cols = slice(head * HD, (head + 1) * HD)
        kv_send[head, :HALF, :] = jnp.concatenate([k_ref[:HALF, cols], k_ref[HALF:, cols]], axis=1)
        kv_send[head, HALF : HALF + HD, :] = v_t[cols, :HALF]
        kv_send[head, HALF + HD :, :] = v_t[cols, HALF:]

    def own_head(zz):
        return 3 * (zz // 2) + 2 * lax.rem(zz, 2)

    def shared_head(zz):
        return 3 * (zz // 2) + 1

    def shared_step(i):
        return jnp.where(lax.rem(z + i, 2) == 0, i, -i)

    def home_step(i):
        return jnp.where(odd == 1, i, -i)

    qb[0] = q_send[own_head(z)]
    qb[8] = q_send[shared_head(z)]
    kv[OWN, 0, slab] = kv_send[own_head(z)]
    kv[SHARED, 0, slab] = kv_send[shared_head(z)]

    pl.semaphore_wait(barrier, len(peers))

    def q_own_copy(n):
        to = along_z(STEPS[n])
        return remote(q_send.at[own_head(to)], qb.at[n], q_ssem.at[n], q_rsem.at[n], dev(x, to, c))

    def q_shared_copy(i):
        to = along_z(shared_step(i))
        return remote(
            q_send.at[shared_head(to)], qb.at[8 + i], q_ssem.at[8 + i], q_rsem.at[8 + i], dev(x, to, c)
        )

    def own_z_copy(n, step):
        to = along_z(step)
        return remote(
            kv_send.at[own_head(to)], kv.at[OWN, n, slab], z_ssem.at[OWN, n], z_rsem.at[OWN, n], dev(x, to, c)
        )

    def shared_z_copy(i):
        to = along_z(shared_step(i))
        return remote(
            kv_send.at[shared_head(to)], kv.at[SHARED, 2 * i, slab],
            z_ssem.at[SHARED, i], z_rsem.at[SHARED, i], dev(x, to, c),
        )

    def partner_copy(i):
        return remote(
            kv.at[SHARED, 2 * i, slab], kv.at[SHARED, 2 * i + 1, slab], p_ssem.at[i], p_rsem.at[i], partner
        )

    def sibling_copy(h, n):
        part = kv.at[h, n, slab]
        return remote(part, part, a_ssem.at[h, n], a_rsem.at[h, n], sibling)

    def across_copy(h, n):
        part = kv.at[h, n, slab]
        return remote(part, part, x_ssem.at[h, n], x_rsem.at[h, n], across)

    def second_copy(h, n):
        part = kv.at[h, n, slab_across]
        return remote(part, part, b_ssem.at[h, n], b_rsem.at[h, n], sibling)

    def spread(h, n):
        across_copy(h, n).start()
        sibling_copy(h, n).start()

    def own_first(n):
        own_z_copy(n, 0).wait_recv()
        spread(OWN, n)

    def shared_first(n):
        if n % 2 == 0:
            shared_z_copy(n // 2).wait_recv()
            partner_copy(n // 2).start()
        else:
            partner_copy(n // 2).wait_recv()
        spread(SHARED, n)

    def second(h, n):
        across_copy(h, n).wait_recv()
        second_copy(h, n).start()

    def arrived(h, n):
        sibling_copy(h, n).wait_recv()
        second_copy(h, n).wait_recv()

    spread(OWN, 0)
    for n in (1, 2):
        own_z_copy(n, STEPS[n]).start()
    for n in range(1, Z):
        q_own_copy(n).start()
    spread(SHARED, 0)
    partner_copy(0).start()
    for n in (3, 4):
        own_z_copy(n, STEPS[n]).start()
    for i in range(1, 4):
        q_shared_copy(i).start()
    for n in (5, 6, 7):
        own_z_copy(n, STEPS[n]).start()

    acc_scr[...] = jnp.zeros_like(acc_scr)
    m_scr[...] = jnp.full_like(m_scr, -1e30)
    ones = jnp.ones((16, CHUNK), BF16)
    zeros = jnp.zeros((HD, ROWS), BF16)

    def scores(h, n, b, slot):
        query = qb[b]
        keys = jnp.concatenate([kv[h, n, s, :HALF, :] for s in range(4)], axis=0)
        top = None
        for half in range(2):
            weight = jnp.concatenate([query, zeros] if half == 0 else [zeros, query], axis=0)
            part = jnp.dot(keys, weight, preferred_element_type=F32)
            s_scr[slot, half * 4 * HALF : (half + 1) * 4 * HALF, :] = part
            part_top = jnp.max(part.reshape(HALF // 2, 8, ROWS), axis=0)
            top = part_top if top is None else jnp.maximum(top, part_top)
        mx_scr[slot] = jnp.max(top, axis=0, keepdims=True) * EXP_SCALE

    def weigh(h, n, b, slot):
        old = m_scr[b]
        new = jnp.maximum(old, mx_scr[slot])
        m_scr[b] = new
        weights, values = [], []
        for half in range(2):
            part = s_scr[slot, half * 4 * HALF : (half + 1) * 4 * HALF, :] * EXP_SCALE - new
            weights.append(jnp.exp2(part).astype(BF16))
            first = HALF + half * HD
            values += [kv[h, n, s, first : first + HD, :] for s in range(4)]
        values = jnp.concatenate([jnp.concatenate(values, axis=1), ones], axis=0)
        product = jnp.dot(values, jnp.concatenate(weights, axis=0), preferred_element_type=F32)
        total = acc_scr[b] * jnp.exp2(old - new) + product
        acc_scr[b] = total
        return total

    def context_copy(b):
        if b < 8:
            to, head = along_z(-STEPS[b]), own_head(z)
        else:
            to, head = along_z(home_step(b - 8)), shared_head(z)
        return remote(ctx_send.at[b], ctx_t.at[head], c_ssem.at[b], c_rsem.at[b], dev(x, to, c))

    def finish(b, total):
        context = (total[:HD] / total[HD : HD + 1]).astype(BF16)
        if b == 0:
            ctx_t[own_head(z)] = context
        elif b == 8:
            ctx_t[shared_head(z)] = context
        else:
            ctx_send[b] = context
            context_copy(b).start()

    shared_units = {3: (0, 1), 9: (2, 4), 10: (6, 3), 11: (5, 7)}

    def place(r, u):
        if isinstance(r, int):
            if r in shared_units:
                return SHARED, shared_units[r][u // 4], 11 - u % 4
            return OWN, r - (r > 3), 7 - u if r == 8 else u
        unit = jnp.where(r == 3, shared_units[3][u // 4], r - jnp.where(r > 3, 1, 0))
        return jnp.where(r == 3, SHARED, OWN), unit, jnp.where(r == 3, 11 - u % 4, u)

    def each(*actions):
        def run():
            for action, *arguments in actions:
                action(*arguments)

        return run

    def q_arrived(*ids):
        for i in ids:
            if i < 8:
                q_own_copy(i).wait_recv()
            else:
                q_shared_copy(i - 8).wait_recv()

    def send_shared():
        for i in range(1, 4):
            shared_z_copy(i).start()

    plan = {
        (0, 0): each((second, OWN, 0), (own_first, 1), (own_first, 2), (arrived, OWN, 0)),
        (0, 1): each((q_arrived, 1, 2)),
        (0, 3): each((q_arrived, 3, 4)),
        (0, 5): each(
            (q_arrived, 5, 6, 7), (second, OWN, 1), (second, OWN, 2), (second, SHARED, 0), (shared_first, 1)
        ),
        (1, 0): each((send_shared,), (arrived, OWN, 1)),
        (2, 0): each((arrived, OWN, 2), (second, SHARED, 1), (own_first, 3)),
        (3, 0): each((own_first, 4), (q_arrived, 9, 10, 11), (arrived, SHARED, 0), (arrived, SHARED, 1)),
        (4, 0): each((second, OWN, 3), (second, OWN, 4), (own_first, 5), (arrived, OWN, 3)),
        (5, 0): each((own_first, 6), (own_first, 7), (arrived, OWN, 4)),
        (6, 0): each((second, OWN, 5), (second, OWN, 6), (shared_first, 2), (arrived, OWN, 5)),
        (7, 0): each((second, OWN, 7), (shared_first, 4), (shared_first, 6), (arrived, OWN, 6)),
        (8, 0): each((second, SHARED, 2), (arrived, OWN, 7)),
        (8, 4): each((shared_first, 3), (shared_first, 5), (second, SHARED, 4)),
        (9, 0): each((second, SHARED, 6), (shared_first, 7), (arrived, SHARED, 2), (arrived, SHARED, 4)),
        (10, 0): each((second, SHARED, 3), (arrived, SHARED, 6)),
        (10, 4): each((second, SHARED, 5), (arrived, SHARED, 3)),
        (11, 0): each((second, SHARED, 7), (arrived, SHARED, 5)),
        (11, 4): each((arrived, SHARED, 7)),
    }

    def steps(r, before):
        for u in range(8):
            if isinstance(r, int):
                if (r, u) in plan:
                    plan[r, u]()
            elif u == 0:
                for at in range(1, 8):
                    pl.when(r == at)(plan[at, 0])
            scores(*place(r, u), u % 2)
            if u > 0 or before is not None:
                previous = place(r, u - 1) if u else place(before, 7)
                weighed(r if u else before, u - 1 if u else 7, weigh(*previous, (u + 1) % 2))

    def weighed(r, u, total):
        if isinstance(r, int) and (r == 8 or (r == 11 and u >= 4)):
            finish(place(r, u)[2], total)

    steps(0, None)

    def one_round(r, carry):
        steps(r, r - 1)
        return carry

    lax.fori_loop(1, 8, one_round, 0)
    for r in (8, 9, 10, 11):
        steps(r, r - 1)
    weighed(11, 7, weigh(*place(11, 7), 1))

    for load in loads[3:]:
        load.wait()

    def project(heads):
        context = jnp.concatenate([ctx_t[h] for h in heads], axis=0).T
        weight = jnp.concatenate([wout[h * HD : (h + 1) * HD, :] for h in heads], axis=0)
        return jnp.dot(context, weight, preferred_element_type=F32)

    for b in range(1, 8):
        context_copy(b).wait_recv()
    residual = frames[...].astype(F32) + project(OWN_HEADS)
    for b in range(9, 12):
        context_copy(b).wait_recv()
    residual = residual + project(SHARED_HEADS)
    att_ref[...] = residual.astype(BF16)
    att_store = pltpu.make_async_copy(att_ref, att_hbm, local_sem.at[0])
    att_store.start()
    centered = residual - jnp.mean(residual, axis=1, keepdims=True)
    variance = jnp.mean(centered * centered, axis=1, keepdims=True)
    gain = gain_ref[...].reshape(1, -1)
    normed = (centered * lax.rsqrt(variance + 1e-05) * gain).astype(BF16)
    projected = jnp.dot(normed, wglu[...], preferred_element_type=F32)
    channels = projected.shape[1] // 2
    gated = (projected[:, :channels] * jax.nn.sigmoid(projected[:, channels:])).astype(BF16)

    halo_send[0] = gated[:EDGE]
    halo_send[1] = gated[ROWS - EDGE :]
    to_left = remote(halo_send.at[0], halo_recv.at[1], h_ssem.at[0], h_rsem.at[1], left)
    to_right = remote(halo_send.at[1], halo_recv.at[0], h_ssem.at[1], h_rsem.at[0], right)
    to_left.start()
    to_right.start()
    gpad[EDGE : EDGE + ROWS, :] = gated.astype(F32)
    bn_scale, bn_shift = bns_ref[...].reshape(1, -1), bnb_ref[...].reshape(1, -1)

    def convolve(first, rows):
        for col in range(0, channels, 128):
            cols = slice(col, col + 128)
            conv = None
            for r in range(8):
                part = None
                for u in range(r, 32, 8):
                    if u == 0:
                        continue
                    begin = first + u - r
                    term = gpad[begin : begin + rows + 8, cols] * dw_ref[u - 1 : u, cols]
                    part = term if part is None else part + term
                taps_tmp[r, : rows + 8] = part
                shifted = taps_tmp[r, r : r + rows, :]
                conv = shifted if conv is None else conv + shifted
            u = bn_scale[:, cols] * conv + bn_shift[:, cols]
            conv_ref[first : first + rows, cols] = (u * jax.nn.sigmoid(u)).astype(BF16)

    def store(first, rows, sem):
        part = pl.ds(first, rows)
        return pltpu.make_async_copy(conv_ref.at[part], conv_hbm.at[part], local_sem.at[sem])

    convolve(EDGE, ROWS - 2 * EDGE)
    inner_store = store(EDGE, ROWS - 2 * EDGE, 1)
    inner_store.start()
    to_left.wait_recv()
    to_right.wait_recv()
    gpad[:EDGE, :] = jnp.where(me == 0, 0.0, halo_recv[0].astype(F32))
    gpad[EDGE + ROWS :, :] = jnp.where(me == 31, 0.0, halo_recv[1].astype(F32))
    convolve(0, EDGE)
    convolve(ROWS - EDGE, EDGE)
    edge_stores = [store(0, EDGE, 2), store(ROWS - EDGE, EDGE, 3)]
    for edge in edge_stores:
        edge.start()

    for n in range(1, Z):
        q_own_copy(n).wait_send()
        own_z_copy(n, STEPS[n]).wait_send()
    for i in range(1, 4):
        q_shared_copy(i).wait_send()
        shared_z_copy(i).wait_send()
    for i in range(4):
        partner_copy(i).wait_send()
    for h in (OWN, SHARED):
        for n in range(Z):
            across_copy(h, n).wait_send()
            sibling_copy(h, n).wait_send()
            second_copy(h, n).wait_send()
    for b in range(12):
        if b not in (0, 8):
            context_copy(b).wait_send()
    to_left.wait_send()
    to_right.wait_send()
    for copy in [att_store, inner_store] + edge_stores:
        copy.wait()


def hand_on(att_in, conv_in, att_out, conv_out, att, conv, in_sem, out_sem):
    rows = ROWS // 4
    copies = []
    for i in range(4):
        part = pl.ds(i * rows, rows)
        for j, (src, held, dst) in enumerate([(att_in, att, att_out), (conv_in, conv, conv_out)]):
            copies.append(
                (
                    pltpu.make_async_copy(src.at[part], held.at[part], in_sem.at[2 * i + j]),
                    pltpu.make_async_copy(held.at[part], dst.at[part], out_sem.at[2 * i + j]),
                )
            )
    for load, store in copies:
        load.start()
    for load, store in copies:
        load.wait()
        store.start()
    for load, store in copies:
        store.wait()


def local(frames_in, queries, keys, values, w_out, ln_gain, w_glu, dw_weight, bn_scale, bn_shift):
    rows, width = frames_in.shape
    channels = w_glu.shape[1] // 2
    hbm = pl.BlockSpec(memory_space=pl.ANY)
    dma = pltpu.SemaphoreType.DMA
    units = [dma((2, Z))] * 8
    out_shape = (
        jax.ShapeDtypeStruct((rows, width), BF16),
        jax.ShapeDtypeStruct((rows, channels), BF16),
    )
    results = pl.pallas_call(
        kernel,
        out_shape=out_shape,
        in_specs=[hbm] * 10,
        out_specs=(hbm, hbm),
        scratch_shapes=[
            pltpu.VMEM(queries.shape, BF16),
            pltpu.VMEM(keys.shape, BF16),
            pltpu.VMEM(values.shape, BF16),
            pltpu.VMEM(ln_gain.shape, F32),
            pltpu.VMEM(dw_weight.shape, F32),
            pltpu.VMEM(bn_scale.shape, F32),
            pltpu.VMEM(bn_shift.shape, F32),
            pltpu.VMEM((rows, width), BF16),
            pltpu.VMEM((rows, channels), BF16),
            pltpu.VMEM((12, ROWS, 128), BF16),
            pltpu.VMEM((12, HD, ROWS), BF16),
            pltpu.VMEM((2, Z, 4, ROWS, 128), BF16),
            pltpu.VMEM((12, HD, ROWS), BF16),
            pltpu.VMEM((12, HD, ROWS), BF16),
            pltpu.VMEM((12, HD, ROWS), BF16),
            pltpu.VMEM((2, CHUNK, ROWS), F32),
            pltpu.VMEM((2, 1, ROWS), F32),
            pltpu.VMEM((12, 1, ROWS), F32),
            pltpu.VMEM((12, HD + 16, ROWS), F32),
            pltpu.VMEM((rows, width), BF16),
            pltpu.VMEM(w_out.shape, BF16),
            pltpu.VMEM(w_glu.shape, BF16),
            pltpu.VMEM((ROWS + 2 * EDGE, channels), F32),
            pltpu.VMEM((8, ROWS + 8, 128), F32),
            pltpu.VMEM((2, EDGE, channels), BF16),
            pltpu.VMEM((2, EDGE, channels), BF16),
            dma((10,)),
            dma((12,)),
            dma((12,)),
        ]
        + units
        + [dma((4,)), dma((4,)), dma((12,)), dma((12,)), dma((2,)), dma((2,))],
        compiler_params=pltpu.CompilerParams(
            collective_id=0, has_side_effects=True, vmem_limit_bytes=56 * 2**20
        ),
    )(frames_in, queries, keys, values, w_out, ln_gain, w_glu, dw_weight, bn_scale, bn_shift)
    return pl.pallas_call(
        hand_on,
        out_shape=out_shape,
        in_specs=[hbm, hbm],
        out_specs=(hbm, hbm),
        scratch_shapes=[
            pltpu.VMEM((rows, width), BF16),
            pltpu.VMEM((rows, channels), BF16),
            dma((8,)),
            dma((8,)),
        ],
    )(*results)


def solution(mesh):
    split = P(("dp", "seq"), None)
    return jax.shard_map(
        local,
        mesh=mesh,
        in_specs=(split,) * 4 + (P(),) * 6,
        out_specs=(split, split),
        check_vma=False,
    )
```

```python
import jax
import jax.numpy as jnp
from jax import lax
from jax.experimental import pallas as pl
from jax.experimental.pallas import tpu as pltpu
from jax.sharding import PartitionSpec as P

MESH = pl.DeviceIdType.MESH
BF16 = jnp.bfloat16
F32 = jnp.float32

HD = 64
TAPS = 31
ROWS = 256
Z = 8
HALF = ROWS // 2
CHUNK = 1024
EXP_SCALE = 0.125 * 1.4426950408889634
OWN_HEADS = (0, 2, 3, 5, 6, 8, 9, 11)
SHARED_HEADS = (1, 4, 7, 10)
EDGE = 16

STEPS = (0, 1, 7, 2, 6, 3, 5, 4)
OWN, SHARED = 0, 1


def kernel(
    frames_hbm, q_hbm, k_hbm, v_hbm, wout_hbm, gain_hbm, wglu_hbm, dw_hbm, bns_hbm, bnb_hbm,
    att_hbm, conv_hbm,
    q_ref, k_ref, v_ref, gain_ref, dw_ref, bns_ref, bnb_ref, att_ref, conv_ref,
    kv_send, q_send, kv, qb, ctx_send, ctx_t, s_scr, mx_scr, m_scr, acc_scr,
    frames, wout, wglu, gpad, taps_tmp, halo_send, halo_recv,
    local_sem, q_ssem, q_rsem, z_ssem, z_rsem, a_ssem, a_rsem, x_ssem, x_rsem, b_ssem, b_rsem,
    p_ssem, p_rsem, c_ssem, c_rsem, h_ssem, h_rsem,
):
    me = lax.axis_index("seq")
    x, z, c = me // 16, lax.rem(me // 2, Z), lax.rem(me, 2)
    odd = lax.rem(z, 2)
    slab, slab_across = 2 * x + c, 2 * (1 - x) + c

    def dev(x, z, c):
        return {"seq": (x * Z + z) * 2 + c}

    def along_z(step):
        return lax.rem(z + step + Z, Z)

    sibling = dev(x, z, 1 - c)
    across = dev(1 - x, z, c)
    partner = dev(x, z + 1 - 2 * odd, c)
    left = {"seq": lax.rem(me + 31, 32)}
    right = {"seq": lax.rem(me + 1, 32)}
    other = {"seq": jnp.where(c == 1, lax.rem(me + 1, 32), lax.rem(me + 31, 32))}

    def remote(src, dst, ssem, rsem, to):
        return pltpu.make_async_remote_copy(
            src_ref=src, dst_ref=dst, send_sem=ssem, recv_sem=rsem, device_id=to, device_id_type=MESH
        )

    barrier = pltpu.get_barrier_semaphore()
    peers = [dev(x, along_z(d), c) for d in (4, 3, 5, 2, 6, 1, 7)] + [sibling, across, other]
    for peer in peers:
        pl.semaphore_signal(barrier, inc=1, device_id=peer, device_id_type=MESH)

    pairs = [
        (q_hbm, q_ref), (v_hbm, v_ref), (k_hbm, k_ref), (frames_hbm, frames), (wout_hbm, wout), (wglu_hbm, wglu),
        (gain_hbm, gain_ref), (dw_hbm, dw_ref), (bns_hbm, bns_ref), (bnb_hbm, bnb_ref),
    ]
    loads = [pltpu.make_async_copy(src, dst, local_sem.at[i]) for i, (src, dst) in enumerate(pairs)]
    for load in loads[:3]:
        load.start()
    for load in loads[:3]:
        load.wait()

    q_send[...] = q_ref[...].T.reshape(q_send.shape)
    v_t = v_ref[...].T
    for head in range(12):
        cols = slice(head * HD, (head + 1) * HD)
        kv_send[head, :HALF, :] = jnp.concatenate([k_ref[:HALF, cols], k_ref[HALF:, cols]], axis=1)
        kv_send[head, HALF : HALF + HD, :] = v_t[cols, :HALF]
        kv_send[head, HALF + HD :, :] = v_t[cols, HALF:]

    def own_head(zz):
        return 3 * (zz // 2) + 2 * lax.rem(zz, 2)

    def shared_head(zz):
        return 3 * (zz // 2) + 1

    def shared_step(i):
        return jnp.where(lax.rem(z + i, 2) == 0, i, -i)

    def home_step(i):
        return jnp.where(odd == 1, i, -i)

    qb[0] = q_send[own_head(z)]
    qb[8] = q_send[shared_head(z)]
    kv[OWN, 0, slab] = kv_send[own_head(z)]
    kv[SHARED, 0, slab] = kv_send[shared_head(z)]

    pl.semaphore_wait(barrier, len(peers))

    def q_own_copy(n):
        to = along_z(STEPS[n])
        return remote(q_send.at[own_head(to)], qb.at[n], q_ssem.at[n], q_rsem.at[n], dev(x, to, c))

    def q_shared_copy(i):
        to = along_z(shared_step(i))
        return remote(
            q_send.at[shared_head(to)], qb.at[8 + i], q_ssem.at[8 + i], q_rsem.at[8 + i], dev(x, to, c)
        )

    def own_z_copy(n, step):
        to = along_z(step)
        return remote(
            kv_send.at[own_head(to)], kv.at[OWN, n, slab], z_ssem.at[OWN, n], z_rsem.at[OWN, n], dev(x, to, c)
        )

    def shared_z_copy(i):
        to = along_z(shared_step(i))
        return remote(
            kv_send.at[shared_head(to)], kv.at[SHARED, 2 * i, slab],
            z_ssem.at[SHARED, i], z_rsem.at[SHARED, i], dev(x, to, c),
        )

    def partner_copy(i):
        return remote(
            kv.at[SHARED, 2 * i, slab], kv.at[SHARED, 2 * i + 1, slab], p_ssem.at[i], p_rsem.at[i], partner
        )

    def sibling_copy(h, n):
        part = kv.at[h, n, slab]
        return remote(part, part, a_ssem.at[h, n], a_rsem.at[h, n], sibling)

    def across_copy(h, n):
        part = kv.at[h, n, slab]
        return remote(part, part, x_ssem.at[h, n], x_rsem.at[h, n], across)

    def second_copy(h, n):
        part = kv.at[h, n, slab_across]
        return remote(part, part, b_ssem.at[h, n], b_rsem.at[h, n], sibling)

    def spread(h, n):
        across_copy(h, n).start()
        sibling_copy(h, n).start()

    def own_first(n):
        own_z_copy(n, 0).wait_recv()
        spread(OWN, n)

    def shared_first(n):
        if n % 2 == 0:
            shared_z_copy(n // 2).wait_recv()
            partner_copy(n // 2).start()
        else:
            partner_copy(n // 2).wait_recv()
        spread(SHARED, n)

    def second(h, n):
        across_copy(h, n).wait_recv()
        second_copy(h, n).start()

    def arrived(h, n):
        sibling_copy(h, n).wait_recv()
        second_copy(h, n).wait_recv()

    spread(OWN, 0)
    for n in (1, 2):
        own_z_copy(n, STEPS[n]).start()
    for n in range(1, Z):
        q_own_copy(n).start()
    spread(SHARED, 0)
    partner_copy(0).start()
    for n in (3, 4):
        own_z_copy(n, STEPS[n]).start()
    for i in range(1, 4):
        q_shared_copy(i).start()
    for n in (5, 6, 7):
        own_z_copy(n, STEPS[n]).start()

    for load in loads[3:]:
        load.start()

    acc_scr[...] = jnp.zeros_like(acc_scr)
    m_scr[...] = jnp.full_like(m_scr, -1e30)
    ones = jnp.ones((16, CHUNK), BF16)
    zeros = jnp.zeros((HD, ROWS), BF16)

    def scores(h, n, b, slot):
        query = qb[b]
        keys = jnp.concatenate([kv[h, n, s, :HALF, :] for s in range(4)], axis=0)
        top = None
        for half in range(2):
            weight = jnp.concatenate([query, zeros] if half == 0 else [zeros, query], axis=0)
            part = jnp.dot(keys, weight, preferred_element_type=F32)
            s_scr[slot, half * 4 * HALF : (half + 1) * 4 * HALF, :] = part
            part_top = jnp.max(part.reshape(HALF // 2, 8, ROWS), axis=0)
            top = part_top if top is None else jnp.maximum(top, part_top)
        mx_scr[slot] = jnp.max(top, axis=0, keepdims=True) * EXP_SCALE

    def weigh(h, n, b, slot):
        old = m_scr[b]
        new = jnp.maximum(old, mx_scr[slot])
        m_scr[b] = new
        weights, values = [], []
        for half in range(2):
            part = s_scr[slot, half * 4 * HALF : (half + 1) * 4 * HALF, :] * EXP_SCALE - new
            weights.append(jnp.exp2(part).astype(BF16))
            first = HALF + half * HD
            values += [kv[h, n, s, first : first + HD, :] for s in range(4)]
        values = jnp.concatenate([jnp.concatenate(values, axis=1), ones], axis=0)
        product = jnp.dot(values, jnp.concatenate(weights, axis=0), preferred_element_type=F32)
        total = acc_scr[b] * jnp.exp2(old - new) + product
        acc_scr[b] = total
        return total

    def context_copy(b):
        if b < 8:
            to, head = along_z(-STEPS[b]), own_head(z)
        else:
            to, head = along_z(home_step(b - 8)), shared_head(z)
        return remote(ctx_send.at[b], ctx_t.at[head], c_ssem.at[b], c_rsem.at[b], dev(x, to, c))

    def finish(b, total):
        context = (total[:HD] / total[HD : HD + 1]).astype(BF16)
        if b == 0:
            ctx_t[own_head(z)] = context
        elif b == 8:
            ctx_t[shared_head(z)] = context
        else:
            ctx_send[b] = context
            context_copy(b).start()

    shared_units = {3: (0, 1), 9: (2, 4), 10: (6, 3), 11: (5, 7)}

    def place(r, u):
        if isinstance(r, int):
            if r in shared_units:
                return SHARED, shared_units[r][u // 4], 11 - u % 4
            return OWN, r - (r > 3), 7 - u if r == 8 else u
        unit = jnp.where(r == 3, shared_units[3][u // 4], r - jnp.where(r > 3, 1, 0))
        return jnp.where(r == 3, SHARED, OWN), unit, jnp.where(r == 3, 11 - u % 4, u)

    def each(*actions):
        def run():
            for action, *arguments in actions:
                action(*arguments)

        return run

    def q_arrived(*ids):
        for i in ids:
            if i < 8:
                q_own_copy(i).wait_recv()
            else:
                q_shared_copy(i - 8).wait_recv()

    def send_shared():
        for i in range(1, 4):
            shared_z_copy(i).start()

    plan = {
        (0, 0): each((second, OWN, 0), (own_first, 1), (own_first, 2), (arrived, OWN, 0)),
        (0, 1): each((q_arrived, 1, 2)),
        (0, 3): each((q_arrived, 3, 4)),
        (0, 5): each(
            (q_arrived, 5, 6, 7), (second, OWN, 1), (second, OWN, 2), (second, SHARED, 0), (shared_first, 1)
        ),
        (1, 0): each((send_shared,), (arrived, OWN, 1)),
        (2, 0): each((arrived, OWN, 2), (second, SHARED, 1), (own_first, 3)),
        (3, 0): each((own_first, 4), (q_arrived, 9, 10, 11), (arrived, SHARED, 0), (arrived, SHARED, 1)),
        (4, 0): each((second, OWN, 3), (second, OWN, 4), (own_first, 5), (arrived, OWN, 3)),
        (5, 0): each((own_first, 6), (own_first, 7), (arrived, OWN, 4)),
        (6, 0): each((second, OWN, 5), (second, OWN, 6), (shared_first, 2), (arrived, OWN, 5)),
        (7, 0): each((second, OWN, 7), (shared_first, 4), (shared_first, 6), (arrived, OWN, 6)),
        (8, 0): each((second, SHARED, 2), (arrived, OWN, 7)),
        (8, 4): each((shared_first, 3), (shared_first, 5), (second, SHARED, 4)),
        (9, 0): each((second, SHARED, 6), (shared_first, 7), (arrived, SHARED, 2), (arrived, SHARED, 4)),
        (10, 0): each((second, SHARED, 3), (arrived, SHARED, 6)),
        (10, 4): each((second, SHARED, 5), (arrived, SHARED, 3)),
        (11, 0): each((second, SHARED, 7), (arrived, SHARED, 5)),
        (11, 4): each((arrived, SHARED, 7)),
    }

    def steps(r, before):
        for u in range(8):
            if isinstance(r, int):
                if (r, u) in plan:
                    plan[r, u]()
            elif u == 0:
                for at in range(1, 8):
                    pl.when(r == at)(plan[at, 0])
            scores(*place(r, u), u % 2)
            if u > 0 or before is not None:
                previous = place(r, u - 1) if u else place(before, 7)
                weighed(r if u else before, u - 1 if u else 7, weigh(*previous, (u + 1) % 2))

    def weighed(r, u, total):
        if isinstance(r, int) and (r == 8 or (r == 11 and u >= 4)):
            finish(place(r, u)[2], total)

    steps(0, None)

    def one_round(r, carry):
        steps(r, r - 1)
        return carry

    lax.fori_loop(1, 8, one_round, 0)
    for r in (8, 9, 10, 11):
        steps(r, r - 1)
    weighed(11, 7, weigh(*place(11, 7), 1))

    for load in loads[3:]:
        load.wait()

    def project(heads):
        context = jnp.concatenate([ctx_t[h] for h in heads], axis=0).T
        weight = jnp.concatenate([wout[h * HD : (h + 1) * HD, :] for h in heads], axis=0)
        return jnp.dot(context, weight, preferred_element_type=F32)

    for b in range(1, 8):
        context_copy(b).wait_recv()
    residual = frames[...].astype(F32) + project(OWN_HEADS)
    for b in range(9, 12):
        context_copy(b).wait_recv()
    residual = residual + project(SHARED_HEADS)
    att_ref[...] = residual.astype(BF16)
    att_store = pltpu.make_async_copy(att_ref, att_hbm, local_sem.at[0])
    att_store.start()
    centered = residual - jnp.mean(residual, axis=1, keepdims=True)
    variance = jnp.mean(centered * centered, axis=1, keepdims=True)
    gain = gain_ref[...].reshape(1, -1)
    normed = (centered * lax.rsqrt(variance + 1e-05) * gain).astype(BF16)
    channels = wglu.shape[1] // 2
    gated = []
    for col in range(0, channels, 256):
        value = jnp.dot(normed, wglu[:, col : col + 256], preferred_element_type=F32)
        gate = jnp.dot(normed, wglu[:, channels + col : channels + col + 256], preferred_element_type=F32)
        gated.append((value * jax.nn.sigmoid(gate)).astype(BF16))
    gated = jnp.concatenate(gated, axis=1)

    halo_send[0] = gated[:EDGE]
    halo_send[1] = gated[ROWS - EDGE :]
    to_left = remote(halo_send.at[0], halo_recv.at[1], h_ssem.at[0], h_rsem.at[1], left)
    to_right = remote(halo_send.at[1], halo_recv.at[0], h_ssem.at[1], h_rsem.at[0], right)
    to_left.start()
    to_right.start()
    gpad[EDGE : EDGE + ROWS, :] = gated.astype(F32)
    bn_scale, bn_shift = bns_ref[...].reshape(1, -1), bnb_ref[...].reshape(1, -1)

    def convolve(first, rows):
        for col in range(0, channels, 128):
            cols = slice(col, col + 128)
            conv = None
            for r in range(8):
                part = None
                for u in range(r, 32, 8):
                    if u == 0:
                        continue
                    begin = first + u - r
                    term = gpad[begin : begin + rows + 8, cols] * dw_ref[u - 1 : u, cols]
                    part = term if part is None else part + term
                held = taps_tmp.at[col // 128, r]
                held[first : first + rows + 8, :] = part
                shifted = held[first + r : first + r + rows, :]
                conv = shifted if conv is None else conv + shifted
            u = bn_scale[:, cols] * conv + bn_shift[:, cols]
            conv_ref[first : first + rows, cols] = (u * jax.nn.sigmoid(u)).astype(BF16)

    def store(first, rows, sem):
        part = pl.ds(first, rows)
        return pltpu.make_async_copy(conv_ref.at[part], conv_hbm.at[part], local_sem.at[sem])

    convolve(EDGE, ROWS - 2 * EDGE)
    inner_store = store(EDGE, ROWS - 2 * EDGE, 1)
    inner_store.start()
    to_left.wait_recv()
    to_right.wait_recv()
    gpad[:EDGE, :] = jnp.where(me == 0, 0.0, halo_recv[0].astype(F32))
    gpad[EDGE + ROWS :, :] = jnp.where(me == 31, 0.0, halo_recv[1].astype(F32))
    convolve(0, EDGE)
    convolve(ROWS - EDGE, EDGE)
    edge_stores = [store(0, EDGE, 2), store(ROWS - EDGE, EDGE, 3)]
    for edge in edge_stores:
        edge.start()

    for n in range(1, Z):
        q_own_copy(n).wait_send()
        own_z_copy(n, STEPS[n]).wait_send()
    for i in range(1, 4):
        q_shared_copy(i).wait_send()
        shared_z_copy(i).wait_send()
    for i in range(4):
        partner_copy(i).wait_send()
    for h in (OWN, SHARED):
        for n in range(Z):
            across_copy(h, n).wait_send()
            sibling_copy(h, n).wait_send()
            second_copy(h, n).wait_send()
    for b in range(12):
        if b not in (0, 8):
            context_copy(b).wait_send()
    to_left.wait_send()
    to_right.wait_send()
    for copy in [att_store, inner_store] + edge_stores:
        copy.wait()


def hand_on(att_in, conv_in, att_out, conv_out, att, conv, in_sem, out_sem):
    rows = ROWS // 4
    copies = []
    for i in range(4):
        part = pl.ds(i * rows, rows)
        for j, (src, held, dst) in enumerate([(att_in, att, att_out), (conv_in, conv, conv_out)]):
            copies.append(
                (
                    pltpu.make_async_copy(src.at[part], held.at[part], in_sem.at[2 * i + j]),
                    pltpu.make_async_copy(held.at[part], dst.at[part], out_sem.at[2 * i + j]),
                )
            )
    for load, store in copies:
        load.start()
    for load, store in copies:
        load.wait()
        store.start()
    for load, store in copies:
        store.wait()


def local(frames_in, queries, keys, values, w_out, ln_gain, w_glu, dw_weight, bn_scale, bn_shift):
    rows, width = frames_in.shape
    channels = w_glu.shape[1] // 2
    hbm = pl.BlockSpec(memory_space=pl.ANY)
    dma = pltpu.SemaphoreType.DMA
    units = [dma((2, Z))] * 8
    out_shape = (
        jax.ShapeDtypeStruct((rows, width), BF16),
        jax.ShapeDtypeStruct((rows, channels), BF16),
    )
    results = pl.pallas_call(
        kernel,
        out_shape=out_shape,
        in_specs=[hbm] * 10,
        out_specs=(hbm, hbm),
        scratch_shapes=[
            pltpu.VMEM(queries.shape, BF16),
            pltpu.VMEM(keys.shape, BF16),
            pltpu.VMEM(values.shape, BF16),
            pltpu.VMEM(ln_gain.shape, F32),
            pltpu.VMEM(dw_weight.shape, F32),
            pltpu.VMEM(bn_scale.shape, F32),
            pltpu.VMEM(bn_shift.shape, F32),
            pltpu.VMEM((rows, width), BF16),
            pltpu.VMEM((rows, channels), BF16),
            pltpu.VMEM((12, ROWS, 128), BF16),
            pltpu.VMEM((12, HD, ROWS), BF16),
            pltpu.VMEM((2, Z, 4, ROWS, 128), BF16),
            pltpu.VMEM((12, HD, ROWS), BF16),
            pltpu.VMEM((12, HD, ROWS), BF16),
            pltpu.VMEM((12, HD, ROWS), BF16),
            pltpu.VMEM((2, CHUNK, ROWS), F32),
            pltpu.VMEM((2, 1, ROWS), F32),
            pltpu.VMEM((12, 1, ROWS), F32),
            pltpu.VMEM((12, HD + 16, ROWS), F32),
            pltpu.VMEM((rows, width), BF16),
            pltpu.VMEM(w_out.shape, BF16),
            pltpu.VMEM(w_glu.shape, BF16),
            pltpu.VMEM((ROWS + 2 * EDGE, channels), F32),
            pltpu.VMEM((channels // 128, 8, ROWS + 8, 128), F32),
            pltpu.VMEM((2, EDGE, channels), BF16),
            pltpu.VMEM((2, EDGE, channels), BF16),
            dma((10,)),
            dma((12,)),
            dma((12,)),
        ]
        + units
        + [dma((4,)), dma((4,)), dma((12,)), dma((12,)), dma((2,)), dma((2,))],
        compiler_params=pltpu.CompilerParams(
            collective_id=0, has_side_effects=True, vmem_limit_bytes=56 * 2**20
        ),
    )(frames_in, queries, keys, values, w_out, ln_gain, w_glu, dw_weight, bn_scale, bn_shift)
    return pl.pallas_call(
        hand_on,
        out_shape=out_shape,
        in_specs=[hbm, hbm],
        out_specs=(hbm, hbm),
        scratch_shapes=[
            pltpu.VMEM((rows, width), BF16),
            pltpu.VMEM((rows, channels), BF16),
            dma((8,)),
            dma((8,)),
        ],
    )(*results)


def solution(mesh):
    split = P(("dp", "seq"), None)
    return jax.shard_map(
        local,
        mesh=mesh,
        in_specs=(split,) * 4 + (P(),) * 6,
        out_specs=(split, split),
        check_vma=False,
    )
```
